512 devices in a mesh: row: 32 (over x, z), col: 16 (over y, core).
Axes of the slice: x: 4, y: 8, z: 8, core: 2. Of those that a mesh axis runs over, the one named last changes fastest.
Arguments:
- source_points: bfloat16 [32768, 1024], P(('row', 'col')), as said below
- target_points: bfloat16 [16384, 1024], P(('col', 'row')), may hold values from -0.3125 to 0.3125
- source_logmass: float32 [32768], P('row'), may hold values from -5 to 5
- target_logmass: float32 [16384], P('col'), may hold values from -5 to 5
Outputs:
- source_potential: float32 [32768], P('row')
- target_potential: float32 [16384], P('col')
The draws below stay inside these ranges and needn't reach their ends.
Inputs may be any that keep to these rules, and one draw needn't show every extreme that they name: `source_points`: normally distributed features of scale about 1024 ** -0.5 per entry; rows may differ in scale.
All inputs are finite; a program needn't handle non-finite values.
Results may differ from the reference program's by a relative error of at most 0.0003.
Values may be sent and summed in bfloat16 or wider, within the bound.
No kernel may reach another device: no remote copies, remote signals or barrier semaphores. Data moves between devices by JAX's collectives and lax.ppermute only.
A program may use at most 64 MiB of HBM per device.

```python
import jax
import jax.numpy as jnp
from jax import lax

D = 1024
ROW_DEV = 1024
ITERS = 3
SRC = 32768
TGT = 16384


def draw_source_points(key, part):
    key = jax.random.fold_in(key, 11)
    first = jax.random.fold_in(key, 0)
    values = jax.random.normal(first, (SRC, D), jnp.float32) * D ** (-0.5)
    return values.astype(jnp.bfloat16)


def levels(key, dims, cuts, smallest, high):
    def one(dim, blocks):
        draws = jax.random.uniform(jax.random.fold_in(jax.random.fold_in(key, 6), dim), (blocks,), jnp.float32, smallest / len(cuts), high / len(cuts))
        return jnp.repeat(jnp.exp(draws), dims[dim] // blocks).reshape((-1,) + (1,) * (len(dims) - dim - 1))

    loudness = one(*cuts[0])
    for cut in cuts[1:]:
        loudness = loudness * one(*cut)
    return loudness


def normal_values(rng, shape, deviation, limit, cuts=(), held_as=jnp.bfloat16):
    values = deviation * jax.random.normal(rng, shape, jnp.float32)
    if cuts:
        values = values * levels(rng, shape, cuts, -0.22, 0.18)
    return jnp.clip(values, -limit, limit).astype(held_as)


def setup_inputs(seed: int = 0) -> dict:
    splits = jax.random.split(jax.random.key(seed), 5)
    source_points = draw_source_points(jax.random.fold_in(splits[4], 71), 0)
    target_points = normal_values(splits[1], (TGT, D), (4 * D ** -0.5), 0.3125, ((0, 512),))
    source_logmass = normal_values(splits[2], (SRC,), 1.0, 5.0, ((0, 32),), jnp.float32)
    target_logmass = normal_values(splits[3], (TGT,), 1.0, 5.0, ((0, 16),), jnp.float32)
    return {"source_points": source_points, "target_points": target_points, "source_logmass": source_logmass, "target_logmass": target_logmass}


epsilon = 0.05


def reference(source_points, target_points, source_logmass, target_logmass):
    source_sq = jnp.sum(jnp.square(source_points.astype(jnp.float32)), axis=1)
    target_sq = jnp.sum(jnp.square(target_points.astype(jnp.float32)), axis=1)
    blocks = SRC // ROW_DEV
    point_blocks = source_points.reshape(blocks, ROW_DEV, D)
    sq_blocks = source_sq.reshape(blocks, ROW_DEV)
    mass_blocks = source_logmass.reshape(blocks, ROW_DEV)
    target_potential = jnp.zeros((TGT,), jnp.float32)
    source_potential = jnp.zeros((SRC,), jnp.float32)
    for step in range(ITERS):
        def visit(carry, item, target_potential=target_potential):
            run_max, run_sum = carry
            points, sq_rows, logmass = item
            products = jnp.dot(points, target_points.T, preferred_element_type=jnp.float32)
            cost_tile = sq_rows[:, None] + target_sq[None, :] - 2.0 * products
            scores = target_logmass[None, :] + (target_potential[None, :] - cost_tile) / epsilon
            highest = jnp.max(scores, axis=1)
            totals = jnp.sum(jnp.exp(scores - highest[:, None]), axis=1)
            src_block = -epsilon * (highest + jnp.log(totals))
            weights = logmass[:, None] + (src_block[:, None] - cost_tile) / epsilon
            block_max = jnp.max(weights, axis=0)
            new_max = jnp.maximum(run_max, block_max)
            run_sum = run_sum * jnp.exp(run_max - new_max) + jnp.sum(jnp.exp(weights - new_max[None, :]), axis=0)
            return (new_max, run_sum), src_block

        start = (jnp.full((TGT,), -jnp.inf, jnp.float32), jnp.zeros((TGT,), jnp.float32))
        (col_max, col_sum), src_blocks = lax.scan(visit, start, (point_blocks, sq_blocks, mass_blocks))
        source_potential = src_blocks.reshape(SRC)
        target_potential = -epsilon * (col_max + jnp.log(col_sum))
    return source_potential, target_potential
```

```python
import math

import jax
import jax.numpy as jnp
from jax import lax
from jax.experimental import pallas as pl
from jax.experimental.pallas import tpu as pltpu
from jax.sharding import PartitionSpec as P

ITERS = 3
EPSILON = 0.05
LOG2E = math.log2(math.e)
SCALE = 2.0 / EPSILON * LOG2E
BACK = EPSILON / LOG2E
NX, NZ = 4, 8
N = 1024
LANES = 128
GROUPS = N // LANES
PER_X = GROUPS // NX
F32 = jnp.float32
SMALL = (GROUPS, LANES)


def move_x(values, step):
    pairs = [(x * NZ + z, (x + step) % NX * NZ + z) for x in range(NX) for z in range(NZ)]
    return lax.ppermute(values, "row", pairs)


def gather_targets(points):
    copies = jnp.broadcast_to(points[None], (NZ,) + points.shape)
    lines = [[x * NZ + z for z in range(NZ)] for x in range(NX)]
    mine = lax.all_to_all(copies, "row", 0, 0, axis_index_groups=lines)
    mine = mine.reshape(-1, points.shape[1])
    half = mine.shape[0] // 2
    before, after = move_x(mine, 1), move_x(mine, -1)
    far = jnp.concatenate([move_x(after[:half], -1), move_x(before[half:], 1)], axis=0)
    return mine, after, far, before


def turned(values, back=False):
    x = lax.axis_index("row") // NZ
    out = values
    for s in range(1, NX):
        cut = (NX - s if back else s) * PER_X
        out = jnp.where(x == s, jnp.concatenate([values[cut:], values[:cut]], axis=0), out)
    return out


def merge_all(parts):
    top = jnp.max(parts, axis=0)
    return top + jnp.log2(jnp.sum(jnp.exp2(parts - top[None]), axis=0))


def over_targets(values, tiles, part, flat):
    for r in range(GROUPS):
        flat[:, pl.ds(r * LANES, LANES)] = jnp.broadcast_to(values[r : r + 1], SMALL)
    rows = []
    for r in range(GROUPS):
        tile = jnp.concatenate([ref[pl.ds(r * LANES, LANES), :] for ref in tiles], axis=1)
        tile = tile + flat[0:1, :]
        top = jnp.max(tile, axis=1, keepdims=True)
        log = top + jnp.log2(jnp.sum(jnp.exp2(tile - top), axis=1, keepdims=True))
        rows.append(jnp.broadcast_to(log, (LANES, LANES)).T[0:1])
    part[...] = jnp.broadcast_to(jnp.concatenate(rows, axis=0)[None], part.shape)


def first_kernel(mass, squares, *refs):
    tiles, (part, flat) = refs[:NX], refs[NX:]
    values = turned(mass[...] * LOG2E) - squares[...] * (1.0 / BACK)
    over_targets(values, tiles, part, flat)


def source_kernel(parts, mass, *refs):
    tiles, (part, flat) = refs[:NX], refs[NX:]
    over_targets(turned(mass[...] * LOG2E - merge_all(parts[...])), tiles, part, flat)


def target_kernel(parts, mass, squares, *refs):
    tiles, (part, potential, side) = refs[:NX], refs[NX:]
    log = merge_all(parts[...])
    potential[...] = squares[...] - BACK * log
    values = mass[...] * LOG2E - log
    for r in range(GROUPS):
        block = jnp.broadcast_to(values[r : r + 1], (LANES, LANES)).T
        side[pl.ds(r * LANES, LANES), :] = block
    rows = []
    for r in range(GROUPS):
        at = pl.ds(r % PER_X * LANES, LANES)
        tile = tiles[r // PER_X][:, at] + side[...]
        top = jnp.max(tile, axis=0, keepdims=True)
        rows.append(top + jnp.log2(jnp.sum(jnp.exp2(tile - top), axis=0, keepdims=True)))
    whole = turned(jnp.concatenate(rows, axis=0), back=True)
    part[...] = jnp.broadcast_to(whole[None], part.shape)


def last_kernel(parts, squares, potential):
    potential[...] = turned(squares[...], back=True) - BACK * merge_all(parts[...])


VMEM = pl.BlockSpec(memory_space=pltpu.VMEM)
WIDE = pltpu.VMEM((GROUPS, N), F32)
TALL = pltpu.VMEM((N, LANES), F32)


def call(kernel, shapes, scratch, *args):
    return pl.pallas_call(
        kernel,
        out_shape=[jax.ShapeDtypeStruct(shape, F32) for shape in shapes],
        in_specs=[VMEM] * len(args),
        out_specs=[VMEM] * len(shapes),
        scratch_shapes=scratch,
        compiler_params=pltpu.CompilerParams(vmem_limit_bytes=16 * 2**20),
        cost_estimate=pl.CostEstimate(
            flops=6 * N * N, bytes_accessed=4 * N * N, transcendentals=N * N
        ),
        name=kernel.__name__,
    )(*args)


def products(a, b):
    return SCALE * lax.dot_general(a, b, (((1,), (1,)), ((), ())), preferred_element_type=F32)


def squares(points):
    return jnp.sum(jnp.square(points.astype(F32)), axis=1).reshape(-1, LANES)


def local(source_points, target_points, source_logmass, target_logmass):
    rows, cols = lax.axis_size("row"), lax.axis_size("col")
    source_mass = source_logmass.reshape(SMALL)
    target_mass = target_logmass.reshape(SMALL)
    source = lax.all_gather(source_points, "col", axis=0, tiled=True)
    targets = gather_targets(target_points)
    target_sq = jnp.concatenate([squares(block) for block in targets], axis=0)
    tiles = [products(source, block) for block in targets]
    (part,) = call(first_kernel, [(cols,) + SMALL], [WIDE], target_mass, target_sq, *tiles)
    source_sq = squares(source)
    for step in range(ITERS):
        parts = lax.all_to_all(part, "col", 0, 0)
        part, source_potential = call(
            target_kernel, [(rows,) + SMALL, SMALL], [TALL], parts, source_mass, source_sq, *tiles
        )
        parts = lax.all_to_all(part, "row", 0, 0)
        if step < ITERS - 1:
            (part,) = call(source_kernel, [(cols,) + SMALL], [WIDE], parts, target_mass, *tiles)
    (target_potential,) = call(last_kernel, [SMALL], [], parts, target_sq)
    return source_potential.reshape(-1), target_potential.reshape(-1)


def solution(mesh):
    in_specs = (P(("row", "col"), None), P(("col", "row"), None), P("row"), P("col"))
    out_specs = (P("row"), P("col"))
    return jax.shard_map(local, mesh=mesh, in_specs=in_specs, out_specs=out_specs, check_vma=False)
```

```python
import math

import jax
import jax.numpy as jnp
from jax import lax
from jax.experimental import pallas as pl
from jax.experimental.pallas import tpu as pltpu
from jax.sharding import PartitionSpec as P

ITERS = 3
EPSILON = 0.05
LOG2E = math.log2(math.e)
SCALE = 2.0 / EPSILON * LOG2E
BACK = EPSILON / LOG2E
NX, NZ, NY, NC = 4, 8, 8, 2
RING = (0, -1, 1, -2, 2, -3, 3, 4)
N = 1024
LANES = 128
GROUPS = N // LANES
F32 = jnp.float32
SMALL = (GROUPS, LANES)


def move_col(values, place):
    pairs = []
    for y in range(NY):
        for core in range(NC):
            to_y, to_core = place(y, core)
            pairs.append((y * NC + core, to_y % NY * NC + to_core))
    return lax.ppermute(values, "col", pairs)


def ring_step(ahead, back):
    return (
        move_col(ahead, lambda y, core: (y + 1, core)),
        move_col(back, lambda y, core: (y - 1, core)),
    )


def spread(values, count, lines):
    copies = jnp.broadcast_to(values[None], (count,) + values.shape)
    out = lax.all_to_all(copies, "row", 0, 0, axis_index_groups=lines)
    return out.reshape((-1,) + values.shape[1:])


def gather_points(source_points, target_points, masses):
    along_z = [[x * NZ + z for z in range(NZ)] for x in range(NX)]
    along_x = [[x * NZ + z for x in range(NX)] for z in range(NZ)]
    line = spread(target_points, NZ, along_z)
    held = {0: source_points}
    held[-1], held[1] = ring_step(source_points, source_points)
    held[-2], held[2] = ring_step(held[-1], held[1])
    held[-2], held[2], line, masses = lax.optimization_barrier((held[-2], held[2], line, masses))
    target = spread(line, NX, along_x)
    held[-3], held[3] = ring_step(held[-2], held[2])
    held[4] = move_col(held[3], lambda y, core: (y - 1, core))
    mine = assemble([held[place] for place in RING])
    other = move_col(mine, lambda y, core: (y, 1 - core))
    return mine, other, target, masses


def assemble_kernel(*refs):
    pieces = refs[: len(RING)]
    out, sems = refs[len(RING) :]
    y = lax.axis_index("col") // NC
    made = []
    for k, ref in enumerate(pieces):
        rows = ref.shape[0]
        start = pl.multiple_of((y + RING[k] + NY) % NY * rows, rows)
        made.append(pltpu.make_async_copy(ref, out.at[pl.ds(start, rows)], sems.at[k]))
        made[-1].start()
    for copy in made:
        copy.wait()


def place_kernel(points, out, squares, sems):
    made = []
    for r in range(GROUPS):
        rows = pl.ds(r * LANES, LANES)
        made.append(pltpu.make_async_copy(points.at[rows], out.at[rows], sems.at[r]))
        made[-1].start()
    sums = []
    for r in range(GROUPS):
        made[r].wait()
        square = jnp.square(out[pl.ds(r * LANES, LANES), :].astype(F32))
        total = jnp.sum(square, axis=1, keepdims=True)
        sums.append(jnp.broadcast_to(total, (LANES, LANES)).T[0:1])
    squares[...] = jnp.concatenate(sums, axis=0)


def columns(values, side):
    for r in range(GROUPS):
        side[pl.ds(r * LANES, LANES), :] = jnp.broadcast_to(values[r : r + 1], (LANES, LANES)).T


def by_core(values):
    swapped = jnp.concatenate([values[GROUPS // 2 :], values[: GROUPS // 2]], axis=0)
    core = lax.axis_index("col") % NC
    return jnp.where(core == 1, swapped, values)


def merge_all(parts):
    top = jnp.max(parts, axis=0)
    return top + jnp.log2(jnp.sum(jnp.exp2(parts - top[None]), axis=0))


def over_targets(values, mine, other, part, flat):
    for r in range(GROUPS):
        flat[:, pl.ds(r * LANES, LANES)] = jnp.broadcast_to(values[r : r + 1], SMALL)
    rows = []
    for scaled in (mine, other):
        for r in range(GROUPS // NC):
            tile = scaled[pl.ds(r * LANES, LANES), :] + flat[0:1, :]
            top = jnp.max(tile, axis=1, keepdims=True)
            log = top + jnp.log2(jnp.sum(jnp.exp2(tile - top), axis=1, keepdims=True))
            rows.append(jnp.broadcast_to(log, (LANES, LANES)).T[0:1])
    part[...] = jnp.broadcast_to(by_core(jnp.concatenate(rows, axis=0))[None], part.shape)


def first_kernel(mass, squares, mine, other, part, flat):
    over_targets(mass[...] - squares[...] * (1.0 / BACK), mine, other, part, flat)


def source_kernel(parts, mass, mine, other, part, flat):
    over_targets(mass[...] - merge_all(parts[...]), mine, other, part, flat)


def target_kernel(parts, mass, squares, mine, other, part, potential, side):
    log = merge_all(parts[...])
    potential[...] = by_core(squares[...]) - BACK * log
    columns(by_core(mass[...] - log), side)
    rows = []
    for r in range(GROUPS):
        at = pl.ds(r * LANES, LANES)
        tile = jnp.concatenate([mine[:, at], other[:, at]], axis=0) + side[...]
        top = jnp.max(tile, axis=0, keepdims=True)
        rows.append(top + jnp.log2(jnp.sum(jnp.exp2(tile - top), axis=0, keepdims=True)))
    part[...] = jnp.broadcast_to(jnp.concatenate(rows, axis=0)[None], part.shape)


def last_kernel(parts, squares, potential):
    potential[...] = squares[...] - BACK * merge_all(parts[...])


VMEM = pl.BlockSpec(memory_space=pltpu.VMEM)
HBM = pl.BlockSpec(memory_space=pltpu.HBM)
PARAMS = pltpu.CompilerParams(vmem_limit_bytes=16 * 2**20)
COST = pl.CostEstimate(flops=6 * N * N, bytes_accessed=4 * N * N, transcendentals=N * N)


def assemble(pieces):
    rows, depth = pieces[0].shape
    return pl.pallas_call(
        assemble_kernel,
        out_shape=jax.ShapeDtypeStruct((NY * rows, depth), jnp.bfloat16),
        in_specs=[HBM] * len(RING),
        out_specs=VMEM,
        scratch_shapes=[pltpu.SemaphoreType.DMA((len(RING),))],
        compiler_params=PARAMS,
        cost_estimate=pl.CostEstimate(flops=0, bytes_accessed=2**22, transcendentals=0),
        name="assemble",
    )(*pieces)


WIDE = pltpu.VMEM((GROUPS, N), F32)
TALL = pltpu.VMEM((N, LANES), F32)


def place(points):
    return pl.pallas_call(
        place_kernel,
        out_shape=(
            jax.ShapeDtypeStruct(points.shape, jnp.bfloat16),
            jax.ShapeDtypeStruct(SMALL, F32),
        ),
        in_specs=[HBM],
        out_specs=(VMEM, VMEM),
        scratch_shapes=[pltpu.SemaphoreType.DMA((GROUPS,))],
        compiler_params=PARAMS,
        cost_estimate=COST,
        name="place",
    )(points)


def call(kernel, shapes, scratch, *args):
    return pl.pallas_call(
        kernel,
        out_shape=[jax.ShapeDtypeStruct(shape, F32) for shape in shapes],
        in_specs=[VMEM] * len(args),
        out_specs=[VMEM] * len(shapes),
        scratch_shapes=scratch,
        compiler_params=PARAMS,
        cost_estimate=COST,
        name=kernel.__name__,
    )(*args)


def products(a, b):
    return SCALE * lax.dot_general(a, b, (((1,), (1,)), ((), ())), preferred_element_type=F32)


def squares(points):
    return jnp.sum(jnp.square(points.astype(F32)), axis=1).reshape(-1, LANES)


def core_first(values):
    return values.reshape(NY, NC, -1).transpose(1, 0, 2).reshape(SMALL)


def y_first(values):
    return values.reshape(NC, NY, -1).transpose(1, 0, 2).reshape(-1)


def local(source_points, target_points, source_logmass, target_logmass):
    rows, cols = lax.axis_size("row"), lax.axis_size("col")
    masses = core_first(source_logmass * LOG2E), (target_logmass * LOG2E).reshape(SMALL)
    mine, other, target, masses = gather_points(source_points, target_points, masses)
    source_mass, target_mass = masses
    target, target_sq = place(target)
    tiles = products(mine, target), products(other, target)
    (part,) = call(first_kernel, [(cols,) + SMALL], [WIDE], target_mass, target_sq, *tiles)
    source_sq = jnp.concatenate([squares(mine), squares(other)], axis=0)
    for step in range(ITERS):
        parts = lax.all_to_all(part, "col", 0, 0)
        part, source_potential = call(
            target_kernel, [(rows,) + SMALL, SMALL], [TALL], parts, source_mass, source_sq, *tiles
        )
        parts = lax.all_to_all(part, "row", 0, 0)
        if step < ITERS - 1:
            (part,) = call(source_kernel, [(cols,) + SMALL], [WIDE], parts, target_mass, *tiles)
    (target_potential,) = call(last_kernel, [SMALL], [], parts, target_sq)
    return y_first(source_potential), target_potential.reshape(-1)


def solution(mesh):
    in_specs = (P(("row", "col"), None), P(("col", "row"), None), P("row"), P("col"))
    out_specs = (P("row"), P("col"))
    return jax.shard_map(local, mesh=mesh, in_specs=in_specs, out_specs=out_specs, check_vma=False)
```

```python
import math

import jax
import jax.numpy as jnp
from jax import lax
from jax.experimental import pallas as pl
from jax.experimental.pallas import tpu as pltpu
from jax.sharding import PartitionSpec as P

ITERS = 3
EPSILON = 0.05
LOG2E = math.log2(math.e)
SCALE = 2.0 / EPSILON * LOG2E
BACK = EPSILON / LOG2E
NX, NZ, NY, NC = 4, 8, 8, 2
RING = (0, -1, 1, -2, 2, -3, 3, 4)
N = 1024
LANES = 128
GROUPS = N // LANES
F32 = jnp.float32
SMALL = (GROUPS, LANES)


def move_col(values, place):
    pairs = []
    for y in range(NY):
        for core in range(NC):
            to_y, to_core = place(y, core)
            pairs.append((y * NC + core, to_y % NY * NC + to_core))
    return lax.ppermute(values, "col", pairs)


def ring_step(ahead, back):
    return (
        move_col(ahead, lambda y, core: (y + 1, core)),
        move_col(back, lambda y, core: (y - 1, core)),
    )


def spread(values, count, lines):
    copies = pl.pallas_call(
        copies_kernel,
        out_shape=jax.ShapeDtypeStruct((count,) + values.shape, values.dtype),
        in_specs=[ANY],
        out_specs=ANY,
        scratch_shapes=[pltpu.SemaphoreType.DMA((count,))],
        compiler_params=PARAMS,
        cost_estimate=pl.CostEstimate(flops=0, bytes_accessed=2**22, transcendentals=0),
        name="copies",
    )(values)
    out = lax.all_to_all(copies, "row", 0, 0, axis_index_groups=lines)
    return out.reshape((-1,) + values.shape[1:])


def gather_points(source_points, target_points, masses):
    along_z = [[x * NZ + z for z in range(NZ)] for x in range(NX)]
    along_x = [[x * NZ + z for x in range(NX)] for z in range(NZ)]
    line = spread(target_points, NZ, along_z)
    held = {0: source_points}
    held[-1], held[1] = ring_step(source_points, source_points)
    held[-2], held[2] = ring_step(held[-1], held[1])
    held[-2], held[2], line, masses = lax.optimization_barrier((held[-2], held[2], line, masses))
    target = spread(line, NX, along_x)
    held[-3], held[3] = ring_step(held[-2], held[2])
    held[4] = move_col(held[3], lambda y, core: (y - 1, core))
    mine = assemble([held[place] for place in RING])
    other = move_col(mine, lambda y, core: (y, 1 - core))
    return mine, other, target, masses


def assemble_kernel(*refs):
    pieces = refs[: len(RING)]
    out, sems = refs[len(RING) :]
    y = lax.axis_index("col") // NC
    made = []
    for k, ref in enumerate(pieces):
        rows = ref.shape[0]
        start = pl.multiple_of((y + RING[k] + NY) % NY * rows, rows)
        made.append(pltpu.make_async_copy(ref, out.at[pl.ds(start, rows)], sems.at[k]))
        made[-1].start()
    for copy in made:
        copy.wait()


def copies_kernel(values, out, sems):
    made = [
        pltpu.make_async_copy(values, out.at[k], sems.at[k]) for k in range(out.shape[0])
    ]
    for copy in made:
        copy.start()
    for copy in made:
        copy.wait()


def columns(values, side):
    for r in range(GROUPS):
        side[pl.ds(r * LANES, LANES), :] = jnp.broadcast_to(values[r : r + 1], (LANES, LANES)).T


def by_core(values):
    swapped = jnp.concatenate([values[GROUPS // 2 :], values[: GROUPS // 2]], axis=0)
    core = lax.axis_index("col") % NC
    return jnp.where(core == 1, swapped, values)


def merge_all(parts):
    top = jnp.max(parts, axis=0)
    return top + jnp.log2(jnp.sum(jnp.exp2(parts - top[None]), axis=0))


def over_targets(values, mine, other, part, flat):
    for r in range(GROUPS):
        flat[:, pl.ds(r * LANES, LANES)] = jnp.broadcast_to(values[r : r + 1], SMALL)
    rows = []
    for scaled in (mine, other):
        for r in range(GROUPS // NC):
            tile = scaled[pl.ds(r * LANES, LANES), :] + flat[0:1, :]
            top = jnp.max(tile, axis=1, keepdims=True)
            log = top + jnp.log2(jnp.sum(jnp.exp2(tile - top), axis=1, keepdims=True))
            rows.append(jnp.broadcast_to(log, (LANES, LANES)).T[0:1])
    part[...] = jnp.broadcast_to(by_core(jnp.concatenate(rows, axis=0))[None], part.shape)


def first_kernel(mass, squares, mine, other, part, flat):
    over_targets(mass[...] - squares[...] * (1.0 / BACK), mine, other, part, flat)


def source_kernel(parts, mass, mine, other, part, flat):
    over_targets(mass[...] - merge_all(parts[...]), mine, other, part, flat)


def target_kernel(parts, mass, squares, mine, other, part, potential, side):
    log = merge_all(parts[...])
    potential[...] = by_core(squares[...]) - BACK * log
    columns(by_core(mass[...] - log), side)
    rows = []
    for r in range(GROUPS):
        at = pl.ds(r * LANES, LANES)
        tile = jnp.concatenate([mine[:, at], other[:, at]], axis=0) + side[...]
        top = jnp.max(tile, axis=0, keepdims=True)
        rows.append(top + jnp.log2(jnp.sum(jnp.exp2(tile - top), axis=0, keepdims=True)))
    part[...] = jnp.broadcast_to(jnp.concatenate(rows, axis=0)[None], part.shape)


def last_kernel(parts, squares, potential):
    potential[...] = squares[...] - BACK * merge_all(parts[...])


VMEM = pl.BlockSpec(memory_space=pltpu.VMEM)
HBM = pl.BlockSpec(memory_space=pltpu.HBM)
ANY = pl.BlockSpec(memory_space=pl.ANY)
PARAMS = pltpu.CompilerParams(vmem_limit_bytes=4 * 2**20)
COST = pl.CostEstimate(flops=6 * N * N, bytes_accessed=4 * N * N, transcendentals=N * N)


def assemble(pieces):
    rows, depth = pieces[0].shape
    return pl.pallas_call(
        assemble_kernel,
        out_shape=jax.ShapeDtypeStruct((NY * rows, depth), jnp.bfloat16),
        in_specs=[HBM] * len(RING),
        out_specs=VMEM,
        scratch_shapes=[pltpu.SemaphoreType.DMA((len(RING),))],
        compiler_params=PARAMS,
        cost_estimate=pl.CostEstimate(flops=0, bytes_accessed=2**22, transcendentals=0),
        name="assemble",
    )(*pieces)


WIDE = pltpu.VMEM((GROUPS, N), F32)
TALL = pltpu.VMEM((N, LANES), F32)


def call(kernel, shapes, scratch, *args):
    return pl.pallas_call(
        kernel,
        out_shape=[jax.ShapeDtypeStruct(shape, F32) for shape in shapes],
        in_specs=[VMEM] * len(args),
        out_specs=[VMEM] * len(shapes),
        scratch_shapes=scratch,
        compiler_params=PARAMS,
        cost_estimate=COST,
        name=kernel.__name__,
    )(*args)


def products(a, b):
    return SCALE * lax.dot_general(a, b, (((1,), (1,)), ((), ())), preferred_element_type=F32)


def squares(points):
    return jnp.sum(jnp.square(points.astype(F32)), axis=1).reshape(-1, LANES)


def core_first(values):
    return values.reshape(NY, NC, -1).transpose(1, 0, 2).reshape(SMALL)


def y_first(values):
    return values.reshape(NC, NY, -1).transpose(1, 0, 2).reshape(-1)


def local(source_points, target_points, source_logmass, target_logmass):
    rows, cols = lax.axis_size("row"), lax.axis_size("col")
    masses = core_first(source_logmass * LOG2E), (target_logmass * LOG2E).reshape(SMALL)
    mine, other, target, masses = gather_points(source_points, target_points, masses)
    source_mass, target_mass = masses
    target_sq = squares(target)
    tiles = products(mine, target), products(other, target)
    (part,) = call(first_kernel, [(cols,) + SMALL], [WIDE], target_mass, target_sq, *tiles)
    source_sq = jnp.concatenate([squares(mine), squares(other)], axis=0)
    for step in range(ITERS):
        parts = lax.all_to_all(part, "col", 0, 0)
        part, source_potential = call(
            target_kernel, [(rows,) + SMALL, SMALL], [TALL], parts, source_mass, source_sq, *tiles
        )
        parts = lax.all_to_all(part, "row", 0, 0)
        if step < ITERS - 1:
            (part,) = call(source_kernel, [(cols,) + SMALL], [WIDE], parts, target_mass, *tiles)
    (target_potential,) = call(last_kernel, [SMALL], [], parts, target_sq)
    return y_first(source_potential), target_potential.reshape(-1)


def solution(mesh):
    in_specs = (P(("row", "col"), None), P(("col", "row"), None), P("row"), P("col"))
    out_specs = (P("row"), P("col"))
    return jax.shard_map(local, mesh=mesh, in_specs=in_specs, out_specs=out_specs, check_vma=False)
```

```python
import math

import jax
import jax.numpy as jnp
from jax import lax
from jax.experimental import pallas as pl
from jax.experimental.pallas import tpu as pltpu
from jax.sharding import PartitionSpec as P

ITERS = 3
EPSILON = 0.05
LOG2E = math.log2(math.e)
SCALE = 2.0 / EPSILON * LOG2E
BACK = EPSILON / LOG2E
NX, NZ, NY, NC = 4, 8, 8, 2
RING = (0, -1, 1, -2, 2, -3, 3, 4)
N = 1024
LANES = 128
GROUPS = N // LANES
F32 = jnp.float32
SMALL = (GROUPS, LANES)


def move_col(values, place):
    pairs = []
    for y in range(NY):
        for core in range(NC):
            to_y, to_core = place(y, core)
            pairs.append((y * NC + core, to_y % NY * NC + to_core))
    return lax.ppermute(values, "col", pairs)


def ring_step(ahead, back):
    return (
        move_col(ahead, lambda y, core: (y + 1, core)),
        move_col(back, lambda y, core: (y - 1, core)),
    )


def spread(values, count, lines):
    copies = pl.pallas_call(
        copies_kernel,
        out_shape=jax.ShapeDtypeStruct((count,) + values.shape, values.dtype),
        in_specs=[HBM],
        out_specs=HBM,
        scratch_shapes=[pltpu.SemaphoreType.DMA((count,))],
        compiler_params=PARAMS,
        cost_estimate=pl.CostEstimate(flops=0, bytes_accessed=2**22, transcendentals=0),
        name="copies",
    )(values)
    out = lax.all_to_all(copies, "row", 0, 0, axis_index_groups=lines)
    return out.reshape((-1,) + values.shape[1:])


def gather_points(source_points, target_points, masses):
    along_z = [[x * NZ + z for z in range(NZ)] for x in range(NX)]
    along_x = [[x * NZ + z for x in range(NX)] for z in range(NZ)]
    line = spread(target_points, NZ, along_z)
    held = {0: source_points}
    held[-1], held[1] = ring_step(source_points, source_points)
    held[-2], held[2] = ring_step(held[-1], held[1])
    held[-2], held[2], line, masses = lax.optimization_barrier((held[-2], held[2], line, masses))
    target = spread(line, NX, along_x)
    held[-3], held[3] = ring_step(held[-2], held[2])
    held[4] = move_col(held[3], lambda y, core: (y - 1, core))
    mine = assemble([held[place] for place in RING])
    other = move_col(mine, lambda y, core: (y, 1 - core))
    return mine, other, target, masses


def assemble_kernel(*refs):
    pieces = refs[: len(RING)]
    out, sems = refs[len(RING) :]
    y = lax.axis_index("col") // NC
    made = []
    for k, ref in enumerate(pieces):
        rows = ref.shape[0]
        start = pl.multiple_of((y + RING[k] + NY) % NY * rows, rows)
        made.append(pltpu.make_async_copy(ref, out.at[pl.ds(start, rows)], sems.at[k]))
        made[-1].start()
    for copy in made:
        copy.wait()


def copies_kernel(values, out, sems):
    made = [
        pltpu.make_async_copy(values, out.at[k], sems.at[k]) for k in range(out.shape[0])
    ]
    for copy in made:
        copy.start()
    for copy in made:
        copy.wait()


def place_kernel(points, out, squares, sems):
    made = []
    groups = squares.shape[0]
    for r in range(groups):
        rows = pl.ds(r * LANES, LANES)
        made.append(pltpu.make_async_copy(points.at[rows], out.at[rows], sems.at[r]))
        made[-1].start()
    sums = []
    for r in range(groups):
        made[r].wait()
        square = jnp.square(out[pl.ds(r * LANES, LANES), :].astype(F32))
        total = jnp.sum(square, axis=1, keepdims=True)
        sums.append(jnp.broadcast_to(total, (LANES, LANES)).T[0:1])
    squares[...] = jnp.concatenate(sums, axis=0)


def columns(values, side):
    for r in range(GROUPS):
        side[pl.ds(r * LANES, LANES), :] = jnp.broadcast_to(values[r : r + 1], (LANES, LANES)).T


def by_core(values):
    swapped = jnp.concatenate([values[GROUPS // 2 :], values[: GROUPS // 2]], axis=0)
    core = lax.axis_index("col") % NC
    return jnp.where(core == 1, swapped, values)


def merge_all(parts):
    top = jnp.max(parts, axis=0)
    return top + jnp.log2(jnp.sum(jnp.exp2(parts - top[None]), axis=0))


def over_targets(values, mine, other, part, flat):
    for r in range(GROUPS):
        flat[:, pl.ds(r * LANES, LANES)] = jnp.broadcast_to(values[r : r + 1], SMALL)
    rows = []
    for scaled in (mine, other):
        for r in range(GROUPS // NC):
            tile = scaled[pl.ds(r * LANES, LANES), :] + flat[0:1, :]
            top = jnp.max(tile, axis=1, keepdims=True)
            log = top + jnp.log2(jnp.sum(jnp.exp2(tile - top), axis=1, keepdims=True))
            rows.append(jnp.broadcast_to(log, (LANES, LANES)).T[0:1])
    part[...] = jnp.broadcast_to(by_core(jnp.concatenate(rows, axis=0))[None], part.shape)


def first_kernel(mass, squares, mine, other, part, flat):
    over_targets(mass[...] - squares[...] * (1.0 / BACK), mine, other, part, flat)


def source_kernel(parts, mass, mine, other, part, flat):
    over_targets(mass[...] - merge_all(parts[...]), mine, other, part, flat)


def target_kernel(parts, mass, squares, mine, other, part, potential, side):
    log = merge_all(parts[...])
    potential[...] = by_core(squares[...]) - BACK * log
    columns(by_core(mass[...] - log), side)
    rows = []
    for r in range(GROUPS):
        at = pl.ds(r * LANES, LANES)
        tile = jnp.concatenate([mine[:, at], other[:, at]], axis=0) + side[...]
        top = jnp.max(tile, axis=0, keepdims=True)
        rows.append(top + jnp.log2(jnp.sum(jnp.exp2(tile - top), axis=0, keepdims=True)))
    part[...] = jnp.broadcast_to(jnp.concatenate(rows, axis=0)[None], part.shape)


def last_kernel(parts, squares, potential):
    potential[...] = squares[...] - BACK * merge_all(parts[...])


VMEM = pl.BlockSpec(memory_space=pltpu.VMEM)
HBM = pl.BlockSpec(memory_space=pltpu.HBM)
PARAMS = pltpu.CompilerParams(vmem_limit_bytes=16 * 2**20)
COST = pl.CostEstimate(flops=6 * N * N, bytes_accessed=4 * N * N, transcendentals=N * N)


def assemble(pieces):
    rows, depth = pieces[0].shape
    return pl.pallas_call(
        assemble_kernel,
        out_shape=jax.ShapeDtypeStruct((NY * rows, depth), jnp.bfloat16),
        in_specs=[HBM] * len(RING),
        out_specs=VMEM,
        scratch_shapes=[pltpu.SemaphoreType.DMA((len(RING),))],
        compiler_params=PARAMS,
        cost_estimate=pl.CostEstimate(flops=0, bytes_accessed=2**22, transcendentals=0),
        name="assemble",
    )(*pieces)


WIDE = pltpu.VMEM((GROUPS, N), F32)
TALL = pltpu.VMEM((N, LANES), F32)


def place(points):
    groups = points.shape[0] // LANES
    return pl.pallas_call(
        place_kernel,
        out_shape=(
            jax.ShapeDtypeStruct(points.shape, jnp.bfloat16),
            jax.ShapeDtypeStruct((groups, LANES), F32),
        ),
        in_specs=[HBM],
        out_specs=(VMEM, VMEM),
        scratch_shapes=[pltpu.SemaphoreType.DMA((groups,))],
        compiler_params=PARAMS,
        cost_estimate=pl.CostEstimate(
            flops=2 * points.size, bytes_accessed=2 * points.size, transcendentals=0
        ),
        name="place",
    )(points)


def call(kernel, shapes, scratch, *args):
    return pl.pallas_call(
        kernel,
        out_shape=[jax.ShapeDtypeStruct(shape, F32) for shape in shapes],
        in_specs=[VMEM] * len(args),
        out_specs=[VMEM] * len(shapes),
        scratch_shapes=scratch,
        compiler_params=PARAMS,
        cost_estimate=COST,
        name=kernel.__name__,
    )(*args)


def products(a, b):
    return SCALE * lax.dot_general(a, b, (((1,), (1,)), ((), ())), preferred_element_type=F32)


def squares(points):
    return jnp.sum(jnp.square(points.astype(F32)), axis=1).reshape(-1, LANES)


def core_first(values):
    return values.reshape(NY, NC, -1).transpose(1, 0, 2).reshape(SMALL)


def y_first(values):
    return values.reshape(NC, NY, -1).transpose(1, 0, 2).reshape(-1)


def local(source_points, target_points, source_logmass, target_logmass):
    rows, cols = lax.axis_size("row"), lax.axis_size("col")
    masses = core_first(source_logmass * LOG2E), (target_logmass * LOG2E).reshape(SMALL)
    mine, other, target, masses = gather_points(source_points, target_points, masses)
    source_mass, target_mass = masses
    other, other_sq = place(other)
    source_sq = jnp.concatenate([squares(mine), other_sq], axis=0)
    target, other, source_sq = lax.optimization_barrier((target, other, source_sq))
    target, target_sq = place(target)
    tiles = products(mine, target), products(other, target)
    (part,) = call(first_kernel, [(cols,) + SMALL], [WIDE], target_mass, target_sq, *tiles)
    for step in range(ITERS):
        parts = lax.all_to_all(part, "col", 0, 0)
        part, source_potential = call(
            target_kernel, [(rows,) + SMALL, SMALL], [TALL], parts, source_mass, source_sq, *tiles
        )
        parts = lax.all_to_all(part, "row", 0, 0)
        if step < ITERS - 1:
            (part,) = call(source_kernel, [(cols,) + SMALL], [WIDE], parts, target_mass, *tiles)
    (target_potential,) = call(last_kernel, [SMALL], [], parts, target_sq)
    return y_first(source_potential), target_potential.reshape(-1)


def solution(mesh):
    in_specs = (P(("row", "col"), None), P(("col", "row"), None), P("row"), P("col"))
    out_specs = (P("row"), P("col"))
    return jax.shard_map(local, mesh=mesh, in_specs=in_specs, out_specs=out_specs, check_vma=False)
```

```python
import math

import jax
import jax.numpy as jnp
from jax import lax
from jax.experimental import pallas as pl
from jax.experimental.pallas import tpu as pltpu
from jax.sharding import PartitionSpec as P

ITERS = 3
EPSILON = 0.05
LOG2E = math.log2(math.e)
SCALE = 2.0 / EPSILON * LOG2E
BACK = EPSILON / LOG2E
NX, NZ, NY, NC = 4, 8, 8, 2
RING = (0, -1, 1, -2, 2, -3, 3, 4)
N = 1024
LANES = 128
GROUPS = N // LANES
F32 = jnp.float32
SMALL = (GROUPS, LANES)


def move_col(values, place):
    pairs = []
    for y in range(NY):
        for core in range(NC):
            to_y, to_core = place(y, core)
            pairs.append((y * NC + core, to_y % NY * NC + to_core))
    return lax.ppermute(values, "col", pairs)


def ring_step(ahead, back):
    return (
        move_col(ahead, lambda y, core: (y + 1, core)),
        move_col(back, lambda y, core: (y - 1, core)),
    )


def spread(values, count, lines):
    copies = pl.pallas_call(
        copies_kernel,
        out_shape=jax.ShapeDtypeStruct((count,) + values.shape, values.dtype),
        in_specs=[HBM],
        out_specs=HBM,
        scratch_shapes=[pltpu.SemaphoreType.DMA((count,))],
        compiler_params=PARAMS,
        cost_estimate=pl.CostEstimate(flops=0, bytes_accessed=2**22, transcendentals=0),
        name="copies",
    )(values)
    out = lax.all_to_all(copies, "row", 0, 0, axis_index_groups=lines)
    return out.reshape((-1,) + values.shape[1:])


def gather_points(source_points, target_points, masses):
    along_z = [[x * NZ + z for z in range(NZ)] for x in range(NX)]
    along_x = [[x * NZ + z for x in range(NX)] for z in range(NZ)]
    line = spread(target_points, NZ, along_z)
    held = {0: source_points}
    held[-1], held[1] = ring_step(source_points, source_points)
    held[-2], held[2] = ring_step(held[-1], held[1])
    held[-2], held[2], line, masses = lax.optimization_barrier((held[-2], held[2], line, masses))
    target = spread(line, NX, along_x)
    held[-3], held[3] = ring_step(held[-2], held[2])
    held[4] = move_col(held[3], lambda y, core: (y - 1, core))
    mine = assemble([held[place] for place in RING])
    other = move_col(mine, lambda y, core: (y, 1 - core))
    return mine, other, target, masses


def assemble_kernel(*refs):
    pieces = refs[: len(RING)]
    out, sems = refs[len(RING) :]
    y = lax.axis_index("col") // NC
    made = []
    for k, ref in enumerate(pieces):
        rows = ref.shape[0]
        start = pl.multiple_of((y + RING[k] + NY) % NY * rows, rows)
        made.append(pltpu.make_async_copy(ref, out.at[pl.ds(start, rows)], sems.at[k]))
        made[-1].start()
    for copy in made:
        copy.wait()


def copies_kernel(values, out, sems):
    made = [
        pltpu.make_async_copy(values, out.at[k], sems.at[k]) for k in range(out.shape[0])
    ]
    for copy in made:
        copy.start()
    for copy in made:
        copy.wait()


def place_kernel(points, out, squares, sems):
    made = []
    groups = squares.shape[0]
    for r in range(groups):
        rows = pl.ds(r * LANES, LANES)
        made.append(pltpu.make_async_copy(points.at[rows], out.at[rows], sems.at[r]))
        made[-1].start()
    sums = []
    for r in range(groups):
        made[r].wait()
        square = jnp.square(out[pl.ds(r * LANES, LANES), :].astype(F32))
        total = jnp.sum(square, axis=1, keepdims=True)
        sums.append(jnp.broadcast_to(total, (LANES, LANES)).T[0:1])
    squares[...] = jnp.concatenate(sums, axis=0)


def squares_kernel(points, same, squares):
    sums = []
    for r in range(GROUPS):
        square = jnp.square(points[pl.ds(r * LANES, LANES), :].astype(F32))
        total = jnp.sum(square, axis=1, keepdims=True)
        sums.append(jnp.broadcast_to(total, (LANES, LANES)).T[0:1])
    squares[...] = jnp.concatenate(sums, axis=0)


def columns(values, side):
    for r in range(GROUPS):
        side[pl.ds(r * LANES, LANES), :] = jnp.broadcast_to(values[r : r + 1], (LANES, LANES)).T


def by_core(values):
    swapped = jnp.concatenate([values[GROUPS // 2 :], values[: GROUPS // 2]], axis=0)
    core = lax.axis_index("col") % NC
    return jnp.where(core == 1, swapped, values)


def merge_all(parts):
    top = jnp.max(parts, axis=0)
    return top + jnp.log2(jnp.sum(jnp.exp2(parts - top[None]), axis=0))


def over_targets(values, mine, other, part, flat):
    for r in range(GROUPS):
        flat[:, pl.ds(r * LANES, LANES)] = jnp.broadcast_to(values[r : r + 1], SMALL)
    down = lax.broadcasted_iota(jnp.int32, (LANES, LANES), 0)
    across = lax.broadcasted_iota(jnp.int32, (LANES, LANES), 1)
    rows = []
    for scaled in (mine, other):
        for r in range(GROUPS // NC):
            logs = []
            for start in range(r * LANES, (r + 1) * LANES, 32):
                tile = scaled[pl.ds(start, 32), :] + flat[0:1, :]
                top = jnp.max(tile, axis=1, keepdims=True)
                logs.append(top + jnp.log2(jnp.sum(jnp.exp2(tile - top), axis=1, keepdims=True)))
            log = jnp.where(down == across, jnp.concatenate(logs, axis=0), 0.0)
            rows.append(jnp.sum(log, axis=0, keepdims=True))
    part[...] = by_core(jnp.concatenate(rows, axis=0))


def first_kernel(mass, squares, mine, other, part, flat):
    over_targets(mass[...] - squares[...] * (1.0 / BACK), mine, other, part, flat)


def source_kernel(parts, mass, mine, other, part, flat):
    over_targets(mass[...] - merge_all(parts[...]), mine, other, part, flat)


def target_kernel(parts, mass, squares, mine, other, part, potential, side):
    log = merge_all(parts[...])
    potential[...] = by_core(squares[...]) - BACK * log
    columns(by_core(mass[...] - log), side)
    rows = []
    for r in range(GROUPS):
        at = pl.ds(r * LANES, LANES)
        tops, sums = [], []
        for half, scaled in enumerate((mine, other)):
            for start in range(0, N // NC, 256):
                tile = scaled[pl.ds(start, 256), at] + side[pl.ds(half * N // NC + start, 256), :]
                tops.append(jnp.max(tile, axis=0, keepdims=True))
                sums.append(jnp.sum(jnp.exp2(tile - tops[-1]), axis=0, keepdims=True))
        top = tops[0]
        for other_top in tops[1:]:
            top = jnp.maximum(top, other_top)
        total = sum(s * jnp.exp2(t - top) for s, t in zip(sums, tops))
        rows.append(top + jnp.log2(total))
    part[...] = jnp.broadcast_to(jnp.concatenate(rows, axis=0)[None], part.shape)


def last_kernel(parts, squares, potential):
    potential[...] = squares[...] - BACK * merge_all(parts[...])


VMEM = pl.BlockSpec(memory_space=pltpu.VMEM)
HBM = pl.BlockSpec(memory_space=pltpu.HBM)
PARAMS = pltpu.CompilerParams(vmem_limit_bytes=16 * 2**20)
COST = pl.CostEstimate(flops=6 * N * N, bytes_accessed=4 * N * N, transcendentals=N * N)


def assemble(pieces):
    rows, depth = pieces[0].shape
    return pl.pallas_call(
        assemble_kernel,
        out_shape=jax.ShapeDtypeStruct((NY * rows, depth), jnp.bfloat16),
        in_specs=[HBM] * len(RING),
        out_specs=VMEM,
        scratch_shapes=[pltpu.SemaphoreType.DMA((len(RING),))],
        compiler_params=PARAMS,
        cost_estimate=pl.CostEstimate(flops=0, bytes_accessed=2**22, transcendentals=0),
        name="assemble",
    )(*pieces)


WIDE = pltpu.VMEM((GROUPS, N), F32)
TALL = pltpu.VMEM((N, LANES), F32)


def place(points):
    groups = points.shape[0] // LANES
    return pl.pallas_call(
        place_kernel,
        out_shape=(
            jax.ShapeDtypeStruct(points.shape, jnp.bfloat16),
            jax.ShapeDtypeStruct((groups, LANES), F32),
        ),
        in_specs=[HBM],
        out_specs=(VMEM, VMEM),
        scratch_shapes=[pltpu.SemaphoreType.DMA((groups,))],
        compiler_params=PARAMS,
        cost_estimate=pl.CostEstimate(
            flops=2 * points.size, bytes_accessed=2 * points.size, transcendentals=0
        ),
        name="place",
    )(points)


def in_place_squares(points):
    return pl.pallas_call(
        squares_kernel,
        out_shape=(
            jax.ShapeDtypeStruct(points.shape, jnp.bfloat16),
            jax.ShapeDtypeStruct(SMALL, F32),
        ),
        in_specs=[VMEM],
        out_specs=(VMEM, VMEM),
        input_output_aliases={0: 0},
        compiler_params=PARAMS,
        cost_estimate=COST,
        name="in_place_squares",
    )(points)


def call(kernel, shapes, scratch, *args):
    return pl.pallas_call(
        kernel,
        out_shape=[jax.ShapeDtypeStruct(shape, F32) for shape in shapes],
        in_specs=[VMEM] * len(args),
        out_specs=[VMEM] * len(shapes),
        scratch_shapes=scratch,
        compiler_params=PARAMS,
        cost_estimate=COST,
        name=kernel.__name__,
    )(*args)


def exchange_col(part):
    there = move_col(part, lambda y, core: (y, 1 - core))
    top = jnp.maximum(part, there)
    merged = top + jnp.log2(jnp.exp2(part - top) + jnp.exp2(there - top))
    lines = [[y * NC + core for y in range(NY)] for core in range(NC)]
    copies = jnp.broadcast_to(merged[None], (NY,) + SMALL)
    return lax.all_to_all(copies, "col", 0, 0, axis_index_groups=lines)


def products(a, b):
    return SCALE * lax.dot_general(a, b, (((1,), (1,)), ((), ())), preferred_element_type=F32)


def squares(points):
    return jnp.sum(jnp.square(points.astype(F32)), axis=1).reshape(-1, LANES)


def core_first(values):
    return values.reshape(NY, NC, -1).transpose(1, 0, 2).reshape(SMALL)


def y_first(values):
    return values.reshape(NC, NY, -1).transpose(1, 0, 2).reshape(-1)


def local(source_points, target_points, source_logmass, target_logmass):
    rows = lax.axis_size("row")
    masses = core_first(source_logmass * LOG2E), (target_logmass * LOG2E).reshape(SMALL)
    mine, other, target, masses = gather_points(source_points, target_points, masses)
    source_mass, target_mass = masses
    other, other_sq = place(other)
    source_sq = jnp.concatenate([squares(mine), other_sq], axis=0)
    target, other, source_sq = lax.optimization_barrier((target, other, source_sq))
    target, target_sq = in_place_squares(target)
    tiles = products(mine, target), products(other, target)
    (part,) = call(first_kernel, [SMALL], [WIDE], target_mass, target_sq, *tiles)
    for step in range(ITERS):
        parts = exchange_col(part)
        part, source_potential = call(
            target_kernel, [(rows,) + SMALL, SMALL], [TALL], parts, source_mass, source_sq, *tiles
        )
        parts = lax.all_to_all(part, "row", 0, 0)
        if step < ITERS - 1:
            (part,) = call(source_kernel, [SMALL], [WIDE], parts, target_mass, *tiles)
    (target_potential,) = call(last_kernel, [SMALL], [], parts, target_sq)
    return y_first(source_potential), target_potential.reshape(-1)


def solution(mesh):
    in_specs = (P(("row", "col"), None), P(("col", "row"), None), P("row"), P("col"))
    out_specs = (P("row"), P("col"))
    return jax.shard_map(local, mesh=mesh, in_specs=in_specs, out_specs=out_specs, check_vma=False)
```

```python
import math

import jax
import jax.numpy as jnp
from jax import lax
from jax.experimental import pallas as pl
from jax.experimental.pallas import tpu as pltpu
from jax.sharding import PartitionSpec as P

ITERS = 3
EPSILON = 0.05
LOG2E = math.log2(math.e)
SCALE = 2.0 / EPSILON * LOG2E
BACK = EPSILON / LOG2E
NX, NZ, NY, NC = 4, 8, 8, 2
RING = (0, -1, 1, -2, 2, -3, 3, 4)
N = 1024
LANES = 128
GROUPS = N // LANES
F32 = jnp.float32
SMALL = (GROUPS, LANES)


def move_col(values, place):
    pairs = []
    for y in range(NY):
        for core in range(NC):
            to_y, to_core = place(y, core)
            pairs.append((y * NC + core, to_y % NY * NC + to_core))
    return lax.ppermute(values, "col", pairs)


def ring_step(ahead, back):
    return (
        move_col(ahead, lambda y, core: (y + 1, core)),
        move_col(back, lambda y, core: (y - 1, core)),
    )


def spread(values, count, lines):
    copies = pl.pallas_call(
        copies_kernel,
        out_shape=jax.ShapeDtypeStruct((count,) + values.shape, values.dtype),
        in_specs=[HBM],
        out_specs=HBM,
        scratch_shapes=[pltpu.SemaphoreType.DMA((count,))],
        compiler_params=PARAMS,
        cost_estimate=pl.CostEstimate(flops=0, bytes_accessed=2**22, transcendentals=0),
        name="copies",
    )(values)
    out = lax.all_to_all(copies, "row", 0, 0, axis_index_groups=lines)
    return out.reshape((-1,) + values.shape[1:])


def gather_points(source_points, target_points):
    along_z = [[x * NZ + z for z in range(NZ)] for x in range(NX)]
    along_x = [[x * NZ + z for x in range(NX)] for z in range(NZ)]
    line = spread(target_points, NZ, along_z)
    held = {0: source_points}
    held[4] = move_col(source_points, lambda y, core: (y + 4, core))
    held[-1], held[1] = ring_step(source_points, source_points)
    held[-1], held[1], held[4], line = lax.optimization_barrier(
        (held[-1], held[1], held[4], line)
    )
    target = spread(line, NX, along_x)
    held[-2], held[2] = ring_step(held[-1], held[1])
    held[-3], held[3] = ring_step(held[-2], held[2])
    mine = assemble([held[place] for place in RING])
    other = move_col(mine, lambda y, core: (y, 1 - core))
    return mine, other, target


def assemble_kernel(*refs):
    pieces = refs[: len(RING)]
    out, sems = refs[len(RING) :]
    y = lax.axis_index("col") // NC
    made = []
    for k, ref in enumerate(pieces):
        rows = ref.shape[0]
        start = pl.multiple_of((y + RING[k] + NY) % NY * rows, rows)
        made.append(pltpu.make_async_copy(ref, out.at[pl.ds(start, rows)], sems.at[k]))
        made[-1].start()
    for copy in made:
        copy.wait()


def copies_kernel(values, out, sems):
    made = [
        pltpu.make_async_copy(values, out.at[k], sems.at[k]) for k in range(out.shape[0])
    ]
    for copy in made:
        copy.start()
    for copy in made:
        copy.wait()


def place_kernel(points, out, squares, sems):
    made = []
    groups = squares.shape[0]
    for r in range(groups):
        rows = pl.ds(r * LANES, LANES)
        made.append(pltpu.make_async_copy(points.at[rows], out.at[rows], sems.at[r]))
        made[-1].start()
    sums = []
    for r in range(groups):
        made[r].wait()
        square = jnp.square(out[pl.ds(r * LANES, LANES), :].astype(F32))
        total = jnp.sum(square, axis=1, keepdims=True)
        sums.append(jnp.broadcast_to(total, (LANES, LANES)).T[0:1])
    squares[...] = jnp.concatenate(sums, axis=0)


def squares_kernel(points, same, squares):
    sums = []
    for r in range(GROUPS):
        square = jnp.square(points[pl.ds(r * LANES, LANES), :].astype(F32))
        total = jnp.sum(square, axis=1, keepdims=True)
        sums.append(jnp.broadcast_to(total, (LANES, LANES)).T[0:1])
    squares[...] = jnp.concatenate(sums, axis=0)


def columns(values, side):
    for r in range(GROUPS):
        side[pl.ds(r * LANES, LANES), :] = jnp.broadcast_to(values[r : r + 1], (LANES, LANES)).T


def by_core(values):
    swapped = jnp.concatenate([values[GROUPS // 2 :], values[: GROUPS // 2]], axis=0)
    core = lax.axis_index("col") % NC
    return jnp.where(core == 1, swapped, values)


def merge_all(parts):
    top = jnp.max(parts, axis=0)
    return top + jnp.log2(jnp.sum(jnp.exp2(parts - top[None]), axis=0))


def over_targets(values, mine, other, part, flat):
    for r in range(GROUPS):
        flat[:, pl.ds(r * LANES, LANES)] = jnp.broadcast_to(values[r : r + 1], SMALL)
    rows = []
    for scaled in (mine, other):
        for r in range(GROUPS // NC):
            tile = scaled[pl.ds(r * LANES, LANES), :] + flat[0:1, :]
            top = jnp.max(tile, axis=1, keepdims=True)
            log = top + jnp.log2(jnp.sum(jnp.exp2(tile - top), axis=1, keepdims=True))
            rows.append(jnp.broadcast_to(log, (LANES, LANES)).T[0:1])
    part[...] = jnp.broadcast_to(by_core(jnp.concatenate(rows, axis=0))[None], part.shape)


def first_kernel(mass, squares, mine, other, part, flat):
    over_targets(mass[...] - squares[...] * (1.0 / BACK), mine, other, part, flat)


def source_kernel(parts, mass, mine, other, part, flat):
    over_targets(mass[...] - merge_all(parts[...]), mine, other, part, flat)


def target_kernel(parts, mass, squares, mine, other, part, potential, side):
    log = merge_all(parts[...])
    potential[...] = by_core(squares[...]) - BACK * log
    columns(by_core(mass[...] - log), side)
    rows = []
    for r in range(GROUPS):
        at = pl.ds(r * LANES, LANES)
        tile = jnp.concatenate([mine[:, at], other[:, at]], axis=0) + side[...]
        top = jnp.max(tile, axis=0, keepdims=True)
        rows.append(top + jnp.log2(jnp.sum(jnp.exp2(tile - top), axis=0, keepdims=True)))
    part[...] = jnp.broadcast_to(jnp.concatenate(rows, axis=0)[None], part.shape)


def last_kernel(parts, squares, potential):
    potential[...] = squares[...] - BACK * merge_all(parts[...])


VMEM = pl.BlockSpec(memory_space=pltpu.VMEM)
HBM = pl.BlockSpec(memory_space=pltpu.HBM)
PARAMS = pltpu.CompilerParams(vmem_limit_bytes=16 * 2**20)
COST = pl.CostEstimate(flops=6 * N * N, bytes_accessed=4 * N * N, transcendentals=N * N)


def assemble(pieces):
    rows, depth = pieces[0].shape
    return pl.pallas_call(
        assemble_kernel,
        out_shape=jax.ShapeDtypeStruct((NY * rows, depth), jnp.bfloat16),
        in_specs=[HBM] * len(RING),
        out_specs=VMEM,
        scratch_shapes=[pltpu.SemaphoreType.DMA((len(RING),))],
        compiler_params=PARAMS,
        cost_estimate=pl.CostEstimate(flops=0, bytes_accessed=2**22, transcendentals=0),
        name="assemble",
    )(*pieces)


WIDE = pltpu.VMEM((GROUPS, N), F32)
TALL = pltpu.VMEM((N, LANES), F32)


def place(points):
    groups = points.shape[0] // LANES
    return pl.pallas_call(
        place_kernel,
        out_shape=(
            jax.ShapeDtypeStruct(points.shape, jnp.bfloat16),
            jax.ShapeDtypeStruct((groups, LANES), F32),
        ),
        in_specs=[HBM],
        out_specs=(VMEM, VMEM),
        scratch_shapes=[pltpu.SemaphoreType.DMA((groups,))],
        compiler_params=PARAMS,
        cost_estimate=pl.CostEstimate(
            flops=2 * points.size, bytes_accessed=2 * points.size, transcendentals=0
        ),
        name="place",
    )(points)


def in_place_squares(points):
    return pl.pallas_call(
        squares_kernel,
        out_shape=(
            jax.ShapeDtypeStruct(points.shape, jnp.bfloat16),
            jax.ShapeDtypeStruct(SMALL, F32),
        ),
        in_specs=[VMEM],
        out_specs=(VMEM, VMEM),
        input_output_aliases={0: 0},
        compiler_params=PARAMS,
        cost_estimate=COST,
        name="in_place_squares",
    )(points)


def call(kernel, shapes, scratch, *args):
    return pl.pallas_call(
        kernel,
        out_shape=[jax.ShapeDtypeStruct(shape, F32) for shape in shapes],
        in_specs=[VMEM] * len(args),
        out_specs=[VMEM] * len(shapes),
        scratch_shapes=scratch,
        compiler_params=PARAMS,
        cost_estimate=COST,
        name=kernel.__name__,
    )(*args)


def products(a, b):
    return SCALE * lax.dot_general(a, b, (((1,), (1,)), ((), ())), preferred_element_type=F32)


def squares(points):
    return jnp.sum(jnp.square(points.astype(F32)), axis=1).reshape(-1, LANES)


def core_first(values):
    return values.reshape(NY, NC, -1).transpose(1, 0, 2).reshape(SMALL)


def y_first(values):
    return values.reshape(NC, NY, -1).transpose(1, 0, 2).reshape(-1)


def local(source_points, target_points, source_logmass, target_logmass):
    rows, cols = lax.axis_size("row"), lax.axis_size("col")
    mine, other, target = gather_points(source_points, target_points)
    other, other_sq = place(other)
    source_sq = jnp.concatenate([squares(mine), other_sq], axis=0)
    source_mass = core_first(source_logmass * LOG2E)
    target_mass = (target_logmass * LOG2E).reshape(SMALL)
    target, other, source_sq, source_mass, target_mass = lax.optimization_barrier(
        (target, other, source_sq, source_mass, target_mass)
    )
    target, target_sq = in_place_squares(target)
    tiles = products(mine, target), products(other, target)
    (part,) = call(first_kernel, [(cols,) + SMALL], [WIDE], target_mass, target_sq, *tiles)
    for step in range(ITERS):
        parts = lax.all_to_all(part, "col", 0, 0)
        part, source_potential = call(
            target_kernel, [(rows,) + SMALL, SMALL], [TALL], parts, source_mass, source_sq, *tiles
        )
        parts = lax.all_to_all(part, "row", 0, 0)
        if step < ITERS - 1:
            (part,) = call(source_kernel, [(cols,) + SMALL], [WIDE], parts, target_mass, *tiles)
    (target_potential,) = call(last_kernel, [SMALL], [], parts, target_sq)
    return y_first(source_potential), target_potential.reshape(-1)


def solution(mesh):
    in_specs = (P(("row", "col"), None), P(("col", "row"), None), P("row"), P("col"))
    out_specs = (P("row"), P("col"))
    return jax.shard_map(local, mesh=mesh, in_specs=in_specs, out_specs=out_specs, check_vma=False)
```

```python
import math

import jax
import jax.numpy as jnp
from jax import lax
from jax.experimental import pallas as pl
from jax.experimental.pallas import tpu as pltpu
from jax.sharding import PartitionSpec as P

ITERS = 3
EPSILON = 0.05
LOG2E = math.log2(math.e)
SCALE = 2.0 / EPSILON * LOG2E
BACK = EPSILON / LOG2E
NX, NZ, NY, NC = 4, 8, 8, 2
RING = (0, -1, 1, -2, 2, -3, 3, 4)
N = 1024
LANES = 128
GROUPS = N // LANES
F32 = jnp.float32
SMALL = (GROUPS, LANES)


def move_col(values, place):
    pairs = []
    for y in range(NY):
        for core in range(NC):
            to_y, to_core = place(y, core)
            pairs.append((y * NC + core, to_y % NY * NC + to_core))
    return lax.ppermute(values, "col", pairs)


def ring_step(ahead, back):
    return (
        move_col(ahead, lambda y, core: (y + 1, core)),
        move_col(back, lambda y, core: (y - 1, core)),
    )


def spread(values, count, lines):
    copies = pl.pallas_call(
        copies_kernel,
        out_shape=jax.ShapeDtypeStruct((count,) + values.shape, values.dtype),
        in_specs=[HBM],
        out_specs=HBM,
        scratch_shapes=[pltpu.SemaphoreType.DMA((count, max(1, values.shape[0] // 64)))],
        compiler_params=PARAMS,
        cost_estimate=pl.CostEstimate(flops=0, bytes_accessed=2**22, transcendentals=0),
        name="copies",
    )(values)
    out = lax.all_to_all(copies, "row", 0, 0, axis_index_groups=lines)
    return out.reshape((-1,) + values.shape[1:])


def gather_points(source_points, target_points):
    along_z = [[x * NZ + z for z in range(NZ)] for x in range(NX)]
    along_x = [[x * NZ + z for x in range(NX)] for z in range(NZ)]
    line = spread(target_points, NZ, along_z)
    held = {0: source_points}
    held[-1], held[1] = ring_step(source_points, source_points)
    held[-2], held[2] = ring_step(held[-1], held[1])
    held[-2], held[2], line = lax.optimization_barrier((held[-2], held[2], line))
    target = spread(line, NX, along_x)
    held[-3], held[3] = ring_step(held[-2], held[2])
    held[4] = move_col(held[3], lambda y, core: (y - 1, core))
    mine = assemble([held[place] for place in RING])
    other = move_col(mine, lambda y, core: (y, 1 - core))
    return mine, other, target


def assemble_kernel(*refs):
    pieces = refs[: len(RING)]
    out, sems = refs[len(RING) :]
    y = lax.axis_index("col") // NC
    made = []
    for k, ref in enumerate(pieces):
        rows = ref.shape[0]
        start = pl.multiple_of((y + RING[k] + NY) % NY * rows, rows)
        made.append(pltpu.make_async_copy(ref, out.at[pl.ds(start, rows)], sems.at[k]))
        made[-1].start()
    for copy in made:
        copy.wait()


def copies_kernel(values, out, sems):
    count, parts = sems.shape
    rows = values.shape[0] // parts
    made = [
        pltpu.make_async_copy(
            values.at[pl.ds(part * rows, rows)],
            out.at[k, pl.ds(part * rows, rows)],
            sems.at[k, part],
        )
        for k in range(count)
        for part in range(parts)
    ]
    for copy in made:
        copy.start()
    for copy in made:
        copy.wait()


def place_kernel(points, out, squares, sems):
    made = []
    groups = squares.shape[0]
    for r in range(groups):
        rows = pl.ds(r * LANES, LANES)
        made.append(pltpu.make_async_copy(points.at[rows], out.at[rows], sems.at[r]))
        made[-1].start()
    sums = []
    for r in range(groups):
        made[r].wait()
        square = jnp.square(out[pl.ds(r * LANES, LANES), :].astype(F32))
        total = jnp.sum(square, axis=1, keepdims=True)
        sums.append(jnp.broadcast_to(total, (LANES, LANES)).T[0:1])
    squares[...] = jnp.concatenate(sums, axis=0)


def squares_kernel(points, same, squares):
    sums = []
    for r in range(GROUPS):
        square = jnp.square(points[pl.ds(r * LANES, LANES), :].astype(F32))
        total = jnp.sum(square, axis=1, keepdims=True)
        sums.append(jnp.broadcast_to(total, (LANES, LANES)).T[0:1])
    squares[...] = jnp.concatenate(sums, axis=0)


def columns(values, side):
    for r in range(GROUPS):
        side[pl.ds(r * LANES, LANES), :] = jnp.broadcast_to(values[r : r + 1], (LANES, LANES)).T


def by_core(values):
    swapped = jnp.concatenate([values[GROUPS // 2 :], values[: GROUPS // 2]], axis=0)
    core = lax.axis_index("col") % NC
    return jnp.where(core == 1, swapped, values)


def merge_all(parts):
    top = jnp.max(parts, axis=0)
    return top + jnp.log2(jnp.sum(jnp.exp2(parts - top[None]), axis=0))


def over_targets(values, mine, other, part, flat):
    for r in range(GROUPS):
        flat[:, pl.ds(r * LANES, LANES)] = jnp.broadcast_to(values[r : r + 1], SMALL)
    rows = []
    for scaled in (mine, other):
        for r in range(GROUPS // NC):
            tile = scaled[pl.ds(r * LANES, LANES), :] + flat[0:1, :]
            top = jnp.max(tile, axis=1, keepdims=True)
            log = top + jnp.log2(jnp.sum(jnp.exp2(tile - top), axis=1, keepdims=True))
            rows.append(jnp.broadcast_to(log, (LANES, LANES)).T[0:1])
    part[...] = jnp.broadcast_to(by_core(jnp.concatenate(rows, axis=0))[None], part.shape)


def first_kernel(mass, squares, mine, other, part, flat):
    over_targets(mass[...] - squares[...] * (1.0 / BACK), mine, other, part, flat)


def source_kernel(parts, mass, mine, other, part, flat):
    over_targets(mass[...] - merge_all(parts[...]), mine, other, part, flat)


def target_kernel(parts, mass, squares, mine, other, part, potential, side):
    log = merge_all(parts[...])
    potential[...] = by_core(squares[...]) - BACK * log
    columns(by_core(mass[...] - log), side)
    rows = []
    for r in range(GROUPS):
        at = pl.ds(r * LANES, LANES)
        tile = jnp.concatenate([mine[:, at], other[:, at]], axis=0) + side[...]
        top = jnp.max(tile, axis=0, keepdims=True)
        rows.append(top + jnp.log2(jnp.sum(jnp.exp2(tile - top), axis=0, keepdims=True)))
    part[...] = jnp.broadcast_to(jnp.concatenate(rows, axis=0)[None], part.shape)


def last_kernel(parts, squares, potential):
    potential[...] = squares[...] - BACK * merge_all(parts[...])


VMEM = pl.BlockSpec(memory_space=pltpu.VMEM)
HBM = pl.BlockSpec(memory_space=pltpu.HBM)
PARAMS = pltpu.CompilerParams(vmem_limit_bytes=16 * 2**20)
COST = pl.CostEstimate(flops=6 * N * N, bytes_accessed=4 * N * N, transcendentals=N * N)


def assemble(pieces):
    rows, depth = pieces[0].shape
    return pl.pallas_call(
        assemble_kernel,
        out_shape=jax.ShapeDtypeStruct((NY * rows, depth), jnp.bfloat16),
        in_specs=[HBM] * len(RING),
        out_specs=VMEM,
        scratch_shapes=[pltpu.SemaphoreType.DMA((len(RING),))],
        compiler_params=PARAMS,
        cost_estimate=pl.CostEstimate(flops=0, bytes_accessed=2**22, transcendentals=0),
        name="assemble",
    )(*pieces)


WIDE = pltpu.VMEM((GROUPS, N), F32)
TALL = pltpu.VMEM((N, LANES), F32)


def place(points):
    groups = points.shape[0] // LANES
    return pl.pallas_call(
        place_kernel,
        out_shape=(
            jax.ShapeDtypeStruct(points.shape, jnp.bfloat16),
            jax.ShapeDtypeStruct((groups, LANES), F32),
        ),
        in_specs=[HBM],
        out_specs=(VMEM, VMEM),
        scratch_shapes=[pltpu.SemaphoreType.DMA((groups,))],
        compiler_params=PARAMS,
        cost_estimate=pl.CostEstimate(
            flops=2 * points.size, bytes_accessed=2 * points.size, transcendentals=0
        ),
        name="place",
    )(points)


def in_place_squares(points):
    return pl.pallas_call(
        squares_kernel,
        out_shape=(
            jax.ShapeDtypeStruct(points.shape, jnp.bfloat16),
            jax.ShapeDtypeStruct(SMALL, F32),
        ),
        in_specs=[VMEM],
        out_specs=(VMEM, VMEM),
        input_output_aliases={0: 0},
        compiler_params=PARAMS,
        cost_estimate=COST,
        name="in_place_squares",
    )(points)


def call(kernel, shapes, scratch, *args):
    return pl.pallas_call(
        kernel,
        out_shape=[jax.ShapeDtypeStruct(shape, F32) for shape in shapes],
        in_specs=[VMEM] * len(args),
        out_specs=[VMEM] * len(shapes),
        scratch_shapes=scratch,
        compiler_params=PARAMS,
        cost_estimate=COST,
        name=kernel.__name__,
    )(*args)


def products(a, b):
    return SCALE * lax.dot_general(a, b, (((1,), (1,)), ((), ())), preferred_element_type=F32)


def squares(points):
    return jnp.sum(jnp.square(points.astype(F32)), axis=1).reshape(-1, LANES)


def core_first(values):
    return values.reshape(NY, NC, -1).transpose(1, 0, 2).reshape(SMALL)


def y_first(values):
    return values.reshape(NC, NY, -1).transpose(1, 0, 2).reshape(-1)


def local(source_points, target_points, source_logmass, target_logmass):
    rows, cols = lax.axis_size("row"), lax.axis_size("col")
    mine, other, target = gather_points(source_points, target_points)
    other, other_sq = place(other)
    source_sq = jnp.concatenate([squares(mine), other_sq], axis=0)
    source_mass = core_first(source_logmass * LOG2E)
    target_mass = (target_logmass * LOG2E).reshape(SMALL)
    target, other, source_sq, source_mass, target_mass = lax.optimization_barrier(
        (target, other, source_sq, source_mass, target_mass)
    )
    target, target_sq = in_place_squares(target)
    tiles = products(mine, target), products(other, target)
    (part,) = call(first_kernel, [(cols,) + SMALL], [WIDE], target_mass, target_sq, *tiles)
    for step in range(ITERS):
        parts = lax.all_to_all(part, "col", 0, 0)
        part, source_potential = call(
            target_kernel, [(rows,) + SMALL, SMALL], [TALL], parts, source_mass, source_sq, *tiles
        )
        parts = lax.all_to_all(part, "row", 0, 0)
        if step < ITERS - 1:
            (part,) = call(source_kernel, [(cols,) + SMALL], [WIDE], parts, target_mass, *tiles)
    (target_potential,) = call(last_kernel, [SMALL], [], parts, target_sq)
    return y_first(source_potential), target_potential.reshape(-1)


def solution(mesh):
    in_specs = (P(("row", "col"), None), P(("col", "row"), None), P("row"), P("col"))
    out_specs = (P("row"), P("col"))
    return jax.shard_map(local, mesh=mesh, in_specs=in_specs, out_specs=out_specs, check_vma=False)
```

```python
import math

import jax
import jax.numpy as jnp
from jax import lax
from jax.experimental import pallas as pl
from jax.experimental.pallas import tpu as pltpu
from jax.sharding import PartitionSpec as P

ITERS = 3
EPSILON = 0.05
LOG2E = math.log2(math.e)
SCALE = 2.0 / EPSILON * LOG2E
BACK = EPSILON / LOG2E
NX, NZ, NY, NC = 4, 8, 8, 2
RING = (0, -1, 1, -2, 2, -3, 3, 4)
N = 1024
LANES = 128
GROUPS = N // LANES
F32 = jnp.float32
SMALL = (GROUPS, LANES)


def move_col(values, place):
    pairs = []
    for y in range(NY):
        for core in range(NC):
            to_y, to_core = place(y, core)
            pairs.append((y * NC + core, to_y % NY * NC + to_core))
    return lax.ppermute(values, "col", pairs)


def ring_step(ahead, back):
    return (
        move_col(ahead, lambda y, core: (y + 1, core)),
        move_col(back, lambda y, core: (y - 1, core)),
    )


def spread(values, count, lines):
    copies = pl.pallas_call(
        copies_kernel,
        out_shape=jax.ShapeDtypeStruct((count,) + values.shape, values.dtype),
        in_specs=[HBM],
        out_specs=HBM,
        scratch_shapes=[pltpu.SemaphoreType.DMA((count, max(1, values.shape[0] // 64)))],
        compiler_params=PARAMS,
        cost_estimate=pl.CostEstimate(flops=0, bytes_accessed=2**22, transcendentals=0),
        name="copies",
    )(values)
    out = lax.all_to_all(copies, "row", 0, 0, axis_index_groups=lines)
    return out.reshape((-1,) + values.shape[1:])


def gather_points(source_points, target_points):
    along_z = [[x * NZ + z for z in range(NZ)] for x in range(NX)]
    along_x = [[x * NZ + z for x in range(NX)] for z in range(NZ)]
    line = spread(target_points, NZ, along_z)
    held = {0: source_points}
    held[-1], held[1] = ring_step(source_points, source_points)
    held[-2] = move_col(held[-1], lambda y, core: (y + 1, core))
    held[1], held[-2], line = lax.optimization_barrier((held[1], held[-2], line))
    target = spread(line, NX, along_x)
    held[2] = move_col(held[1], lambda y, core: (y - 1, core))
    held[-3], held[3] = ring_step(held[-2], held[2])
    held[4] = move_col(held[3], lambda y, core: (y - 1, core))
    mine = assemble([held[place] for place in RING])
    other = move_col(mine, lambda y, core: (y, 1 - core))
    return mine, other, target


def assemble_kernel(*refs):
    pieces = refs[: len(RING)]
    out, sems = refs[len(RING) :]
    y = lax.axis_index("col") // NC
    made = []
    for k, ref in enumerate(pieces):
        rows = ref.shape[0]
        start = pl.multiple_of((y + RING[k] + NY) % NY * rows, rows)
        made.append(pltpu.make_async_copy(ref, out.at[pl.ds(start, rows)], sems.at[k]))
        made[-1].start()
    for copy in made:
        copy.wait()


def copies_kernel(values, out, sems):
    count, parts = sems.shape
    rows = values.shape[0] // parts
    made = [
        pltpu.make_async_copy(
            values.at[pl.ds(part * rows, rows)],
            out.at[k, pl.ds(part * rows, rows)],
            sems.at[k, part],
        )
        for k in range(count)
        for part in range(parts)
    ]
    for copy in made:
        copy.start()
    for copy in made:
        copy.wait()


def row_squares(points, groups):
    sums = []
    for r in range(groups):
        square = jnp.square(points[pl.ds(r * LANES, LANES), :].astype(F32))
        total = jnp.sum(square, axis=1, keepdims=True)
        sums.append(jnp.broadcast_to(total, (LANES, LANES)).T[0:1])
    return jnp.concatenate(sums, axis=0)


def settle_kernel(target, other, same, placed, target_sq, other_sq, sems):
    groups = other_sq.shape[0]
    made = []
    for r in range(groups):
        rows = pl.ds(r * LANES, LANES)
        made.append(pltpu.make_async_copy(other.at[rows], placed.at[rows], sems.at[r]))
        made[-1].start()
    target_sq[...] = row_squares(target, target_sq.shape[0])
    for copy in made:
        copy.wait()
    other_sq[...] = row_squares(placed, groups)


def columns(values, side):
    for r in range(GROUPS):
        side[pl.ds(r * LANES, LANES), :] = jnp.broadcast_to(values[r : r + 1], (LANES, LANES)).T


def by_core(values):
    swapped = jnp.concatenate([values[GROUPS // 2 :], values[: GROUPS // 2]], axis=0)
    core = lax.axis_index("col") % NC
    return jnp.where(core == 1, swapped, values)


def merge_all(parts):
    top = jnp.max(parts, axis=0)
    return top + jnp.log2(jnp.sum(jnp.exp2(parts - top[None]), axis=0))


def over_targets(values, mine, other, part, flat):
    for r in range(GROUPS):
        flat[:, pl.ds(r * LANES, LANES)] = jnp.broadcast_to(values[r : r + 1], SMALL)
    rows = []
    for scaled in (mine, other):
        for r in range(GROUPS // NC):
            tile = scaled[pl.ds(r * LANES, LANES), :] + flat[0:1, :]
            top = jnp.max(tile, axis=1, keepdims=True)
            log = top + jnp.log2(jnp.sum(jnp.exp2(tile - top), axis=1, keepdims=True))
            rows.append(jnp.broadcast_to(log, (LANES, LANES)).T[0:1])
    part[...] = jnp.broadcast_to(by_core(jnp.concatenate(rows, axis=0))[None], part.shape)


def first_kernel(mass, squares, mine, other, part, flat):
    over_targets(mass[...] - squares[...] * (1.0 / BACK), mine, other, part, flat)


def source_kernel(parts, mass, mine, other, part, flat):
    over_targets(mass[...] - merge_all(parts[...]), mine, other, part, flat)


def target_kernel(parts, mass, squares, mine, other, part, potential, side):
    log = merge_all(parts[...])
    potential[...] = by_core(squares[...]) - BACK * log
    columns(by_core(mass[...] - log), side)
    rows = []
    for r in range(GROUPS):
        at = pl.ds(r * LANES, LANES)
        tile = jnp.concatenate([mine[:, at], other[:, at]], axis=0) + side[...]
        top = jnp.max(tile, axis=0, keepdims=True)
        rows.append(top + jnp.log2(jnp.sum(jnp.exp2(tile - top), axis=0, keepdims=True)))
    part[...] = jnp.broadcast_to(jnp.concatenate(rows, axis=0)[None], part.shape)


def last_kernel(parts, squares, potential):
    potential[...] = squares[...] - BACK * merge_all(parts[...])


VMEM = pl.BlockSpec(memory_space=pltpu.VMEM)
HBM = pl.BlockSpec(memory_space=pltpu.HBM)
PARAMS = pltpu.CompilerParams(vmem_limit_bytes=16 * 2**20)
COST = pl.CostEstimate(flops=6 * N * N, bytes_accessed=4 * N * N, transcendentals=N * N)


def assemble(pieces):
    rows, depth = pieces[0].shape
    return pl.pallas_call(
        assemble_kernel,
        out_shape=jax.ShapeDtypeStruct((NY * rows, depth), jnp.bfloat16),
        in_specs=[HBM] * len(RING),
        out_specs=VMEM,
        scratch_shapes=[pltpu.SemaphoreType.DMA((len(RING),))],
        compiler_params=PARAMS,
        cost_estimate=pl.CostEstimate(flops=0, bytes_accessed=2**22, transcendentals=0),
        name="assemble",
    )(*pieces)


WIDE = pltpu.VMEM((GROUPS, N), F32)
TALL = pltpu.VMEM((N, LANES), F32)


def settle(target, other):
    groups = other.shape[0] // LANES
    return pl.pallas_call(
        settle_kernel,
        out_shape=(
            jax.ShapeDtypeStruct(target.shape, jnp.bfloat16),
            jax.ShapeDtypeStruct(other.shape, jnp.bfloat16),
            jax.ShapeDtypeStruct(SMALL, F32),
            jax.ShapeDtypeStruct((groups, LANES), F32),
        ),
        in_specs=[VMEM, HBM],
        out_specs=[VMEM] * 4,
        input_output_aliases={0: 0},
        scratch_shapes=[pltpu.SemaphoreType.DMA((groups,))],
        compiler_params=PARAMS,
        cost_estimate=COST,
        name="settle",
    )(target, other)


def call(kernel, shapes, scratch, *args):
    return pl.pallas_call(
        kernel,
        out_shape=[jax.ShapeDtypeStruct(shape, F32) for shape in shapes],
        in_specs=[VMEM] * len(args),
        out_specs=[VMEM] * len(shapes),
        scratch_shapes=scratch,
        compiler_params=PARAMS,
        cost_estimate=COST,
        name=kernel.__name__,
    )(*args)


def products(a, b):
    return SCALE * lax.dot_general(a, b, (((1,), (1,)), ((), ())), preferred_element_type=F32)


def squares(points):
    return jnp.sum(jnp.square(points.astype(F32)), axis=1).reshape(-1, LANES)


def core_first(values):
    return values.reshape(NY, NC, -1).transpose(1, 0, 2).reshape(SMALL)


def y_first(values):
    return values.reshape(NC, NY, -1).transpose(1, 0, 2).reshape(-1)


def local(source_points, target_points, source_logmass, target_logmass):
    rows, cols = lax.axis_size("row"), lax.axis_size("col")
    mine, other, target = gather_points(source_points, target_points)
    mine_sq = squares(mine)
    source_mass = core_first(source_logmass * LOG2E)
    target_mass = (target_logmass * LOG2E).reshape(SMALL)
    target, other, mine_sq, source_mass, target_mass = lax.optimization_barrier(
        (target, other, mine_sq, source_mass, target_mass)
    )
    target, other, target_sq, other_sq = settle(target, other)
    source_sq = jnp.concatenate([mine_sq, other_sq], axis=0)
    tiles = products(mine, target), products(other, target)
    (part,) = call(first_kernel, [(cols,) + SMALL], [WIDE], target_mass, target_sq, *tiles)
    for step in range(ITERS):
        parts = lax.all_to_all(part, "col", 0, 0)
        part, source_potential = call(
            target_kernel, [(rows,) + SMALL, SMALL], [TALL], parts, source_mass, source_sq, *tiles
        )
        parts = lax.all_to_all(part, "row", 0, 0)
        if step < ITERS - 1:
            (part,) = call(source_kernel, [(cols,) + SMALL], [WIDE], parts, target_mass, *tiles)
    (target_potential,) = call(last_kernel, [SMALL], [], parts, target_sq)
    return y_first(source_potential), target_potential.reshape(-1)


def solution(mesh):
    in_specs = (P(("row", "col"), None), P(("col", "row"), None), P("row"), P("col"))
    out_specs = (P("row"), P("col"))
    return jax.shard_map(local, mesh=mesh, in_specs=in_specs, out_specs=out_specs, check_vma=False)
```

```python
import math

import jax
import jax.numpy as jnp
from jax import lax
from jax.experimental import pallas as pl
from jax.experimental.pallas import tpu as pltpu
from jax.sharding import PartitionSpec as P

ITERS = 3
EPSILON = 0.05
LOG2E = math.log2(math.e)
SCALE = 2.0 / EPSILON * LOG2E
BACK = EPSILON / LOG2E
NX, NZ, NY, NC = 4, 8, 8, 2
RING = (0, -1, 1, -2, 2, -3, 3, 4)
N = 1024
LANES = 128
GROUPS = N // LANES
F32 = jnp.float32
SMALL = (GROUPS, LANES)


def move_col(values, place):
    pairs = []
    for y in range(NY):
        for core in range(NC):
            to_y, to_core = place(y, core)
            pairs.append((y * NC + core, to_y % NY * NC + to_core))
    return lax.ppermute(values, "col", pairs)


def ring_step(ahead, back):
    return (
        move_col(ahead, lambda y, core: (y + 1, core)),
        move_col(back, lambda y, core: (y - 1, core)),
    )


def spread(values, count, lines):
    copies = pl.pallas_call(
        copies_kernel,
        out_shape=jax.ShapeDtypeStruct((count,) + values.shape, values.dtype),
        in_specs=[HBM],
        out_specs=HBM,
        scratch_shapes=[pltpu.SemaphoreType.DMA((count,))],
        compiler_params=PARAMS,
        cost_estimate=pl.CostEstimate(flops=0, bytes_accessed=2**22, transcendentals=0),
        name="copies",
    )(values)
    out = lax.all_to_all(copies, "row", 0, 0, axis_index_groups=lines)
    return out.reshape((-1,) + values.shape[1:])


def gather_points(source_points, target_points, masses):
    along_z = [[x * NZ + z for z in range(NZ)] for x in range(NX)]
    along_x = [[x * NZ + z for x in range(NX)] for z in range(NZ)]
    line = spread(target_points, NZ, along_z)
    held = {0: source_points}
    held[-1], held[1] = ring_step(source_points, source_points)
    held[-2], held[2] = ring_step(held[-1], held[1])
    held[-2], held[2], line, masses = lax.optimization_barrier((held[-2], held[2], line, masses))
    target = spread(line, NX, along_x)
    held[-3], held[3] = ring_step(held[-2], held[2])
    held[4] = move_col(held[3], lambda y, core: (y - 1, core))
    mine = assemble([held[place] for place in RING])
    other = move_col(mine, lambda y, core: (y, 1 - core))
    return mine, other, target, masses


def assemble_kernel(*refs):
    pieces = refs[: len(RING)]
    out, sems = refs[len(RING) :]
    y = lax.axis_index("col") // NC
    made = []
    for k, ref in enumerate(pieces):
        rows = ref.shape[0]
        start = pl.multiple_of((y + RING[k] + NY) % NY * rows, rows)
        made.append(pltpu.make_async_copy(ref, out.at[pl.ds(start, rows)], sems.at[k]))
        made[-1].start()
    for copy in made:
        copy.wait()


def copies_kernel(values, out, sems):
    made = [
        pltpu.make_async_copy(values, out.at[k], sems.at[k]) for k in range(out.shape[0])
    ]
    for copy in made:
        copy.start()
    for copy in made:
        copy.wait()


def place_kernel(points, out, squares, sems):
    made = []
    groups = squares.shape[0]
    for r in range(groups):
        rows = pl.ds(r * LANES, LANES)
        made.append(pltpu.make_async_copy(points.at[rows], out.at[rows], sems.at[r]))
        made[-1].start()
    sums = []
    for r in range(groups):
        made[r].wait()
        square = jnp.square(out[pl.ds(r * LANES, LANES), :].astype(F32))
        total = jnp.sum(square, axis=1, keepdims=True)
        sums.append(jnp.broadcast_to(total, (LANES, LANES)).T[0:1])
    squares[...] = jnp.concatenate(sums, axis=0)


def squares_kernel(points, same, squares):
    sums = []
    for r in range(GROUPS):
        square = jnp.square(points[pl.ds(r * LANES, LANES), :].astype(F32))
        total = jnp.sum(square, axis=1, keepdims=True)
        sums.append(jnp.broadcast_to(total, (LANES, LANES)).T[0:1])
    squares[...] = jnp.concatenate(sums, axis=0)


def columns(values, side):
    for r in range(GROUPS):
        side[pl.ds(r * LANES, LANES), :] = jnp.broadcast_to(values[r : r + 1], (LANES, LANES)).T


def by_core(values):
    swapped = jnp.concatenate([values[GROUPS // 2 :], values[: GROUPS // 2]], axis=0)
    core = lax.axis_index("col") % NC
    return jnp.where(core == 1, swapped, values)


def merge_all(parts):
    top = jnp.max(parts, axis=0)
    return top + jnp.log2(jnp.sum(jnp.exp2(parts - top[None]), axis=0))


def over_targets(values, mine, other, part, flat):
    for r in range(GROUPS):
        flat[:, pl.ds(r * LANES, LANES)] = jnp.broadcast_to(values[r : r + 1], SMALL)
    rows = []
    for scaled in (mine, other):
        for r in range(GROUPS // NC):
            tile = scaled[pl.ds(r * LANES, LANES), :] + flat[0:1, :]
            top = jnp.max(tile, axis=1, keepdims=True)
            log = top + jnp.log2(jnp.sum(jnp.exp2(tile - top), axis=1, keepdims=True))
            rows.append(jnp.broadcast_to(log, (LANES, LANES)).T[0:1])
    part[...] = jnp.broadcast_to(by_core(jnp.concatenate(rows, axis=0))[None], part.shape)


def first_kernel(mass, squares, mine, other, part, flat):
    over_targets(mass[...] - squares[...] * (1.0 / BACK), mine, other, part, flat)


def source_kernel(parts, mass, mine, other, part, flat):
    over_targets(mass[...] - merge_all(parts[...]), mine, other, part, flat)


def target_kernel(parts, mass, squares, mine, other, part, potential, side):
    log = merge_all(parts[...])
    potential[...] = by_core(squares[...]) - BACK * log
    columns(by_core(mass[...] - log), side)
    rows = []
    for r in range(GROUPS):
        at = pl.ds(r * LANES, LANES)
        tile = jnp.concatenate([mine[:, at], other[:, at]], axis=0) + side[...]
        top = jnp.max(tile, axis=0, keepdims=True)
        rows.append(top + jnp.log2(jnp.sum(jnp.exp2(tile - top), axis=0, keepdims=True)))
    part[...] = jnp.broadcast_to(jnp.concatenate(rows, axis=0)[None], part.shape)


def last_kernel(parts, squares, potential):
    potential[...] = squares[...] - BACK * merge_all(parts[...])


VMEM = pl.BlockSpec(memory_space=pltpu.VMEM)
HBM = pl.BlockSpec(memory_space=pltpu.HBM)
PARAMS = pltpu.CompilerParams(vmem_limit_bytes=16 * 2**20)
COST = pl.CostEstimate(flops=6 * N * N, bytes_accessed=4 * N * N, transcendentals=N * N)


def assemble(pieces):
    rows, depth = pieces[0].shape
    return pl.pallas_call(
        assemble_kernel,
        out_shape=jax.ShapeDtypeStruct((NY * rows, depth), jnp.bfloat16),
        in_specs=[HBM] * len(RING),
        out_specs=VMEM,
        scratch_shapes=[pltpu.SemaphoreType.DMA((len(RING),))],
        compiler_params=PARAMS,
        cost_estimate=pl.CostEstimate(flops=0, bytes_accessed=2**22, transcendentals=0),
        name="assemble",
    )(*pieces)


WIDE = pltpu.VMEM((GROUPS, N), F32)
TALL = pltpu.VMEM((N, LANES), F32)


def place(points):
    groups = points.shape[0] // LANES
    return pl.pallas_call(
        place_kernel,
        out_shape=(
            jax.ShapeDtypeStruct(points.shape, jnp.bfloat16),
            jax.ShapeDtypeStruct((groups, LANES), F32),
        ),
        in_specs=[HBM],
        out_specs=(VMEM, VMEM),
        scratch_shapes=[pltpu.SemaphoreType.DMA((groups,))],
        compiler_params=PARAMS,
        cost_estimate=pl.CostEstimate(
            flops=2 * points.size, bytes_accessed=2 * points.size, transcendentals=0
        ),
        name="place",
    )(points)


def in_place_squares(points):
    return pl.pallas_call(
        squares_kernel,
        out_shape=(
            jax.ShapeDtypeStruct(points.shape, jnp.bfloat16),
            jax.ShapeDtypeStruct(SMALL, F32),
        ),
        in_specs=[VMEM],
        out_specs=(VMEM, VMEM),
        input_output_aliases={0: 0},
        compiler_params=PARAMS,
        cost_estimate=COST,
        name="in_place_squares",
    )(points)


def call(kernel, shapes, scratch, *args):
    return pl.pallas_call(
        kernel,
        out_shape=[jax.ShapeDtypeStruct(shape, F32) for shape in shapes],
        in_specs=[VMEM] * len(args),
        out_specs=[VMEM] * len(shapes),
        scratch_shapes=scratch,
        compiler_params=PARAMS,
        cost_estimate=COST,
        name=kernel.__name__,
    )(*args)


def products(a, b):
    return SCALE * lax.dot_general(a, b, (((1,), (1,)), ((), ())), preferred_element_type=F32)


def squares(points):
    return jnp.sum(jnp.square(points.astype(F32)), axis=1).reshape(-1, LANES)


def core_first(values):
    return values.reshape(NY, NC, -1).transpose(1, 0, 2).reshape(SMALL)


def y_first(values):
    return values.reshape(NC, NY, -1).transpose(1, 0, 2).reshape(-1)


def local(source_points, target_points, source_logmass, target_logmass):
    rows, cols = lax.axis_size("row"), lax.axis_size("col")
    masses = core_first(source_logmass * LOG2E), (target_logmass * LOG2E).reshape(SMALL)
    mine, other, target, masses = gather_points(source_points, target_points, masses)
    source_mass, target_mass = masses
    other, other_sq = place(other)
    source_sq = jnp.concatenate([squares(mine), other_sq], axis=0)
    target, other, source_sq = lax.optimization_barrier((target, other, source_sq))
    target, target_sq = in_place_squares(target)
    tiles = products(mine, target), products(other, target)
    (part,) = call(first_kernel, [(cols,) + SMALL], [WIDE], target_mass, target_sq, *tiles)
    for step in range(ITERS):
        parts = lax.all_to_all(part, "col", 0, 0)
        part, source_potential = call(
            target_kernel, [(rows,) + SMALL, SMALL], [TALL], parts, source_mass, source_sq, *tiles
        )
        parts = lax.all_to_all(part, "row", 0, 0)
        if step < ITERS - 1:
            (part,) = call(source_kernel, [(cols,) + SMALL], [WIDE], parts, target_mass, *tiles)
    (target_potential,) = call(last_kernel, [SMALL], [], parts, target_sq)
    return y_first(source_potential), target_potential.reshape(-1)


def solution(mesh):
    in_specs = (P(("row", "col"), None), P(("col", "row"), None), P("row"), P("col"))
    out_specs = (P("row"), P("col"))
    return jax.shard_map(local, mesh=mesh, in_specs=in_specs, out_specs=out_specs, check_vma=False)
```

```python
import math

import jax
import jax.numpy as jnp
from jax import lax
from jax.experimental import pallas as pl
from jax.experimental.pallas import tpu as pltpu
from jax.sharding import PartitionSpec as P

ITERS = 3
EPSILON = 0.05
LOG2E = math.log2(math.e)
SCALE = 2.0 / EPSILON * LOG2E
BACK = EPSILON / LOG2E
NX, NZ, NY, NC = 4, 8, 8, 2
N = 1024
LANES = 128
GROUPS = N // LANES
F32 = jnp.float32
SMALL = (GROUPS, LANES)


def move_col(values, place):
    pairs = []
    for y in range(NY):
        for core in range(NC):
            to_y, to_core = place(y, core)
            pairs.append((y * NC + core, to_y % NY * NC + to_core))
    return lax.ppermute(values, "col", pairs)


def move_y(values, steps):
    return move_col(values, lambda y, core: (y + steps, core))


def ring_step(ahead, back):
    return move_y(ahead, 1), move_y(back, -1)


def spread(values, count, lines):
    copies = pl.pallas_call(
        copies_kernel,
        out_shape=jax.ShapeDtypeStruct((count,) + values.shape, values.dtype),
        in_specs=[HBM],
        out_specs=HBM,
        scratch_shapes=[pltpu.SemaphoreType.DMA((count,))],
        compiler_params=PARAMS,
        cost_estimate=pl.CostEstimate(flops=0, bytes_accessed=2**22, transcendentals=0),
        name="copies",
    )(values)
    out = lax.all_to_all(copies, "row", 0, 0, axis_index_groups=lines)
    return out.reshape((-1,) + values.shape[1:])


def gather_points(source_points, target_points, masses):
    along_z = [[x * NZ + z for z in range(NZ)] for x in range(NX)]
    along_x = [[x * NZ + z for x in range(NX)] for z in range(NZ)]
    line = spread(target_points, NZ, along_z)
    before, after = ring_step(source_points, source_points)
    before, after, line, masses = lax.optimization_barrier((before, after, line, masses))
    target = spread(line, NX, along_x)
    half = source_points.shape[0] // 2
    two_before = move_y(jnp.concatenate([source_points, before], axis=0), 2)
    two_after = move_y(jnp.concatenate([source_points, after], axis=0), -2)
    far_low, far_high = move_y(after[:half], -3), move_y(before[half:], 3)
    mine = assemble([source_points, before, after, two_before, two_after, far_low, far_high])
    other = move_col(mine, lambda y, core: (y, 1 - core))
    return mine, other, target, masses


def assemble_kernel(*refs):
    pieces, (out, sems) = refs[:7], refs[7:]
    rows = pieces[0].shape[0]
    half = rows // 2
    moves = [(0, 0, 0, 0), (1, 0, -1, 0), (2, 0, 1, 0), (3, 0, -2, 0), (3, rows, -3, 0)]
    moves += [(4, 0, 2, 0), (4, rows, 3, 0), (5, 0, 4, 0), (6, 0, 4, half)]
    y = lax.axis_index("col") // NC
    made = []
    for k, (piece, first, place, offset) in enumerate(moves):
        size = min(rows, pieces[piece].shape[0])
        start = pl.multiple_of((y + place + NY) % NY * rows + offset, half)
        made.append(
            pltpu.make_async_copy(
                pieces[piece].at[pl.ds(first, size)], out.at[pl.ds(start, size)], sems.at[k]
            )
        )
        made[-1].start()
    for copy in made:
        copy.wait()


def copies_kernel(values, out, sems):
    made = [
        pltpu.make_async_copy(values, out.at[k], sems.at[k]) for k in range(out.shape[0])
    ]
    for copy in made:
        copy.start()
    for copy in made:
        copy.wait()


def place_kernel(points, out, squares, sems):
    made = []
    groups = squares.shape[0]
    for r in range(groups):
        rows = pl.ds(r * LANES, LANES)
        made.append(pltpu.make_async_copy(points.at[rows], out.at[rows], sems.at[r]))
        made[-1].start()
    sums = []
    for r in range(groups):
        made[r].wait()
        square = jnp.square(out[pl.ds(r * LANES, LANES), :].astype(F32))
        total = jnp.sum(square, axis=1, keepdims=True)
        sums.append(jnp.broadcast_to(total, (LANES, LANES)).T[0:1])
    squares[...] = jnp.concatenate(sums, axis=0)


def squares_kernel(points, same, squares):
    sums = []
    for r in range(GROUPS):
        square = jnp.square(points[pl.ds(r * LANES, LANES), :].astype(F32))
        total = jnp.sum(square, axis=1, keepdims=True)
        sums.append(jnp.broadcast_to(total, (LANES, LANES)).T[0:1])
    squares[...] = jnp.concatenate(sums, axis=0)


def columns(values, side):
    for r in range(GROUPS):
        side[pl.ds(r * LANES, LANES), :] = jnp.broadcast_to(values[r : r + 1], (LANES, LANES)).T


def by_core(values):
    swapped = jnp.concatenate([values[GROUPS // 2 :], values[: GROUPS // 2]], axis=0)
    core = lax.axis_index("col") % NC
    return jnp.where(core == 1, swapped, values)


def merge_all(parts):
    top = jnp.max(parts, axis=0)
    return top + jnp.log2(jnp.sum(jnp.exp2(parts - top[None]), axis=0))


def over_targets(values, mine, other, part, flat):
    for r in range(GROUPS):
        flat[:, pl.ds(r * LANES, LANES)] = jnp.broadcast_to(values[r : r + 1], SMALL)
    rows = []
    for scaled in (mine, other):
        for r in range(GROUPS // NC):
            tile = scaled[pl.ds(r * LANES, LANES), :] + flat[0:1, :]
            top = jnp.max(tile, axis=1, keepdims=True)
            log = top + jnp.log2(jnp.sum(jnp.exp2(tile - top), axis=1, keepdims=True))
            rows.append(jnp.broadcast_to(log, (LANES, LANES)).T[0:1])
    part[...] = jnp.broadcast_to(by_core(jnp.concatenate(rows, axis=0))[None], part.shape)


def first_kernel(mass, squares, mine, other, part, flat):
    over_targets(mass[...] - squares[...] * (1.0 / BACK), mine, other, part, flat)


def source_kernel(parts, mass, mine, other, part, flat):
    over_targets(mass[...] - merge_all(parts[...]), mine, other, part, flat)


def target_kernel(parts, mass, squares, mine, other, part, potential, side):
    log = merge_all(parts[...])
    potential[...] = by_core(squares[...]) - BACK * log
    columns(by_core(mass[...] - log), side)
    rows = []
    for r in range(GROUPS):
        at = pl.ds(r * LANES, LANES)
        tile = jnp.concatenate([mine[:, at], other[:, at]], axis=0) + side[...]
        top = jnp.max(tile, axis=0, keepdims=True)
        rows.append(top + jnp.log2(jnp.sum(jnp.exp2(tile - top), axis=0, keepdims=True)))
    part[...] = jnp.broadcast_to(jnp.concatenate(rows, axis=0)[None], part.shape)


def last_kernel(parts, squares, potential):
    potential[...] = squares[...] - BACK * merge_all(parts[...])


VMEM = pl.BlockSpec(memory_space=pltpu.VMEM)
HBM = pl.BlockSpec(memory_space=pltpu.HBM)
PARAMS = pltpu.CompilerParams(vmem_limit_bytes=16 * 2**20)
COST = pl.CostEstimate(flops=6 * N * N, bytes_accessed=4 * N * N, transcendentals=N * N)


def assemble(pieces):
    rows, depth = pieces[0].shape
    return pl.pallas_call(
        assemble_kernel,
        out_shape=jax.ShapeDtypeStruct((NY * rows, depth), jnp.bfloat16),
        in_specs=[HBM] * len(pieces),
        out_specs=VMEM,
        scratch_shapes=[pltpu.SemaphoreType.DMA((9,))],
        compiler_params=PARAMS,
        cost_estimate=pl.CostEstimate(flops=0, bytes_accessed=2**22, transcendentals=0),
        name="assemble",
    )(*pieces)


WIDE = pltpu.VMEM((GROUPS, N), F32)
TALL = pltpu.VMEM((N, LANES), F32)


def place(points):
    groups = points.shape[0] // LANES
    return pl.pallas_call(
        place_kernel,
        out_shape=(
            jax.ShapeDtypeStruct(points.shape, jnp.bfloat16),
            jax.ShapeDtypeStruct((groups, LANES), F32),
        ),
        in_specs=[HBM],
        out_specs=(VMEM, VMEM),
        scratch_shapes=[pltpu.SemaphoreType.DMA((groups,))],
        compiler_params=PARAMS,
        cost_estimate=pl.CostEstimate(
            flops=2 * points.size, bytes_accessed=2 * points.size, transcendentals=0
        ),
        name="place",
    )(points)


def in_place_squares(points):
    return pl.pallas_call(
        squares_kernel,
        out_shape=(
            jax.ShapeDtypeStruct(points.shape, jnp.bfloat16),
            jax.ShapeDtypeStruct(SMALL, F32),
        ),
        in_specs=[VMEM],
        out_specs=(VMEM, VMEM),
        input_output_aliases={0: 0},
        compiler_params=PARAMS,
        cost_estimate=COST,
        name="in_place_squares",
    )(points)


def call(kernel, shapes, scratch, *args):
    return pl.pallas_call(
        kernel,
        out_shape=[jax.ShapeDtypeStruct(shape, F32) for shape in shapes],
        in_specs=[VMEM] * len(args),
        out_specs=[VMEM] * len(shapes),
        scratch_shapes=scratch,
        compiler_params=PARAMS,
        cost_estimate=COST,
        name=kernel.__name__,
    )(*args)


def products(a, b):
    return SCALE * lax.dot_general(a, b, (((1,), (1,)), ((), ())), preferred_element_type=F32)


def squares(points):
    return jnp.sum(jnp.square(points.astype(F32)), axis=1).reshape(-1, LANES)


def core_first(values):
    return values.reshape(NY, NC, -1).transpose(1, 0, 2).reshape(SMALL)


def y_first(values):
    return values.reshape(NC, NY, -1).transpose(1, 0, 2).reshape(-1)


def local(source_points, target_points, source_logmass, target_logmass):
    rows, cols = lax.axis_size("row"), lax.axis_size("col")
    masses = core_first(source_logmass * LOG2E), (target_logmass * LOG2E).reshape(SMALL)
    mine, other, target, masses = gather_points(source_points, target_points, masses)
    source_mass, target_mass = masses
    other, other_sq = place(other)
    source_sq = jnp.concatenate([squares(mine), other_sq], axis=0)
    target, other, source_sq = lax.optimization_barrier((target, other, source_sq))
    target, target_sq = in_place_squares(target)
    tiles = products(mine, target), products(other, target)
    (part,) = call(first_kernel, [(cols,) + SMALL], [WIDE], target_mass, target_sq, *tiles)
    for step in range(ITERS):
        parts = lax.all_to_all(part, "col", 0, 0)
        part, source_potential = call(
            target_kernel, [(rows,) + SMALL, SMALL], [TALL], parts, source_mass, source_sq, *tiles
        )
        parts = lax.all_to_all(part, "row", 0, 0)
        if step < ITERS - 1:
            (part,) = call(source_kernel, [(cols,) + SMALL], [WIDE], parts, target_mass, *tiles)
    (target_potential,) = call(last_kernel, [SMALL], [], parts, target_sq)
    return y_first(source_potential), target_potential.reshape(-1)


def solution(mesh):
    in_specs = (P(("row", "col"), None), P(("col", "row"), None), P("row"), P("col"))
    out_specs = (P("row"), P("col"))
    return jax.shard_map(local, mesh=mesh, in_specs=in_specs, out_specs=out_specs, check_vma=False)
```

```python
import math

import jax
import jax.numpy as jnp
from jax import lax
from jax.experimental import pallas as pl
from jax.experimental.pallas import tpu as pltpu
from jax.sharding import PartitionSpec as P

ITERS = 3
EPSILON = 0.05
LOG2E = math.log2(math.e)
SCALE = 2.0 / EPSILON * LOG2E
BACK = EPSILON / LOG2E
NX, NZ, NY, NC = 4, 8, 8, 2
N = 1024
LANES = 128
GROUPS = N // LANES
F32 = jnp.float32
SMALL = (GROUPS, LANES)


def move_col(values, place):
    pairs = []
    for y in range(NY):
        for core in range(NC):
            to_y, to_core = place(y, core)
            pairs.append((y * NC + core, to_y % NY * NC + to_core))
    return lax.ppermute(values, "col", pairs)


def move_y(values, steps):
    return move_col(values, lambda y, core: (y + steps, core))


def ring_step(ahead, back):
    return move_y(ahead, 1), move_y(back, -1)


def spread(values, count, lines):
    copies = pl.pallas_call(
        copies_kernel,
        out_shape=jax.ShapeDtypeStruct((count,) + values.shape, values.dtype),
        in_specs=[HBM],
        out_specs=HBM,
        scratch_shapes=[pltpu.SemaphoreType.DMA((count,))],
        compiler_params=PARAMS,
        cost_estimate=pl.CostEstimate(flops=0, bytes_accessed=2**22, transcendentals=0),
        name="copies",
    )(values)
    out = lax.all_to_all(copies, "row", 0, 0, axis_index_groups=lines)
    return out.reshape((-1,) + values.shape[1:])


def gather_points(source_points, target_points, masses):
    along_z = [[x * NZ + z for z in range(NZ)] for x in range(NX)]
    along_x = [[x * NZ + z for x in range(NX)] for z in range(NZ)]
    line = spread(target_points, NZ, along_z)
    before, after = ring_step(source_points, source_points)
    before_2, after_2 = move_y(source_points, 2), move_y(source_points, -2)
    before, after, before_2, after_2, line, masses = lax.optimization_barrier(
        (before, after, before_2, after_2, line, masses)
    )
    target = spread(line, NX, along_x)
    half = source_points.shape[0] // 2
    before_3, after_3 = move_y(before, 2), move_y(after, -2)
    far_low, far_high = move_y(after[:half], -3), move_y(before[half:], 3)
    near = [source_points, before, after, before_2, after_2, before_3, after_3]
    mine = assemble(near + [far_low, far_high])
    other = move_col(mine, lambda y, core: (y, 1 - core))
    return mine, other, target, masses


def assemble_kernel(*refs):
    pieces, (out, sems) = refs[:9], refs[9:]
    rows = pieces[0].shape[0]
    half = rows // 2
    places = (0, -1, 1, -2, 2, -3, 3)
    moves = [(k, 0, place, 0) for k, place in enumerate(places)]
    moves += [(7, 0, 4, 0), (8, 0, 4, half)]
    y = lax.axis_index("col") // NC
    made = []
    for k, (piece, first, place, offset) in enumerate(moves):
        size = min(rows, pieces[piece].shape[0])
        start = pl.multiple_of((y + place + NY) % NY * rows + offset, half)
        made.append(
            pltpu.make_async_copy(
                pieces[piece].at[pl.ds(first, size)], out.at[pl.ds(start, size)], sems.at[k]
            )
        )
        made[-1].start()
    for copy in made:
        copy.wait()


def copies_kernel(values, out, sems):
    made = [
        pltpu.make_async_copy(values, out.at[k], sems.at[k]) for k in range(out.shape[0])
    ]
    for copy in made:
        copy.start()
    for copy in made:
        copy.wait()


def place_kernel(points, out, squares, sems):
    made = []
    groups = squares.shape[0]
    for r in range(groups):
        rows = pl.ds(r * LANES, LANES)
        made.append(pltpu.make_async_copy(points.at[rows], out.at[rows], sems.at[r]))
        made[-1].start()
    sums = []
    for r in range(groups):
        made[r].wait()
        square = jnp.square(out[pl.ds(r * LANES, LANES), :].astype(F32))
        total = jnp.sum(square, axis=1, keepdims=True)
        sums.append(jnp.broadcast_to(total, (LANES, LANES)).T[0:1])
    squares[...] = jnp.concatenate(sums, axis=0)


def squares_kernel(points, same, squares):
    sums = []
    for r in range(GROUPS):
        square = jnp.square(points[pl.ds(r * LANES, LANES), :].astype(F32))
        total = jnp.sum(square, axis=1, keepdims=True)
        sums.append(jnp.broadcast_to(total, (LANES, LANES)).T[0:1])
    squares[...] = jnp.concatenate(sums, axis=0)


def columns(values, side):
    for r in range(GROUPS):
        side[pl.ds(r * LANES, LANES), :] = jnp.broadcast_to(values[r : r + 1], (LANES, LANES)).T


def by_core(values):
    swapped = jnp.concatenate([values[GROUPS // 2 :], values[: GROUPS // 2]], axis=0)
    core = lax.axis_index("col") % NC
    return jnp.where(core == 1, swapped, values)


def merge_all(parts):
    top = jnp.max(parts, axis=0)
    return top + jnp.log2(jnp.sum(jnp.exp2(parts - top[None]), axis=0))


def over_targets(values, mine, other, part, flat):
    for r in range(GROUPS):
        flat[:, pl.ds(r * LANES, LANES)] = jnp.broadcast_to(values[r : r + 1], SMALL)
    rows = []
    for scaled in (mine, other):
        for r in range(GROUPS // NC):
            tile = scaled[pl.ds(r * LANES, LANES), :] + flat[0:1, :]
            top = jnp.max(tile, axis=1, keepdims=True)
            log = top + jnp.log2(jnp.sum(jnp.exp2(tile - top), axis=1, keepdims=True))
            rows.append(jnp.broadcast_to(log, (LANES, LANES)).T[0:1])
    part[...] = jnp.broadcast_to(by_core(jnp.concatenate(rows, axis=0))[None], part.shape)


def first_kernel(mass, squares, mine, other, part, flat):
    over_targets(mass[...] - squares[...] * (1.0 / BACK), mine, other, part, flat)


def source_kernel(parts, mass, mine, other, part, flat):
    over_targets(mass[...] - merge_all(parts[...]), mine, other, part, flat)


def target_kernel(parts, mass, squares, mine, other, part, potential, side):
    log = merge_all(parts[...])
    potential[...] = by_core(squares[...]) - BACK * log
    columns(by_core(mass[...] - log), side)
    rows = []
    for r in range(GROUPS):
        at = pl.ds(r * LANES, LANES)
        tile = jnp.concatenate([mine[:, at], other[:, at]], axis=0) + side[...]
        top = jnp.max(tile, axis=0, keepdims=True)
        rows.append(top + jnp.log2(jnp.sum(jnp.exp2(tile - top), axis=0, keepdims=True)))
    part[...] = jnp.broadcast_to(jnp.concatenate(rows, axis=0)[None], part.shape)


def last_kernel(parts, squares, potential):
    potential[...] = squares[...] - BACK * merge_all(parts[...])


VMEM = pl.BlockSpec(memory_space=pltpu.VMEM)
HBM = pl.BlockSpec(memory_space=pltpu.HBM)
PARAMS = pltpu.CompilerParams(vmem_limit_bytes=16 * 2**20)
COST = pl.CostEstimate(flops=6 * N * N, bytes_accessed=4 * N * N, transcendentals=N * N)


def assemble(pieces):
    rows, depth = pieces[0].shape
    return pl.pallas_call(
        assemble_kernel,
        out_shape=jax.ShapeDtypeStruct((NY * rows, depth), jnp.bfloat16),
        in_specs=[HBM] * len(pieces),
        out_specs=VMEM,
        scratch_shapes=[pltpu.SemaphoreType.DMA((9,))],
        compiler_params=PARAMS,
        cost_estimate=pl.CostEstimate(flops=0, bytes_accessed=2**22, transcendentals=0),
        name="assemble",
    )(*pieces)


WIDE = pltpu.VMEM((GROUPS, N), F32)
TALL = pltpu.VMEM((N, LANES), F32)


def place(points):
    groups = points.shape[0] // LANES
    return pl.pallas_call(
        place_kernel,
        out_shape=(
            jax.ShapeDtypeStruct(points.shape, jnp.bfloat16),
            jax.ShapeDtypeStruct((groups, LANES), F32),
        ),
        in_specs=[HBM],
        out_specs=(VMEM, VMEM),
        scratch_shapes=[pltpu.SemaphoreType.DMA((groups,))],
        compiler_params=PARAMS,
        cost_estimate=pl.CostEstimate(
            flops=2 * points.size, bytes_accessed=2 * points.size, transcendentals=0
        ),
        name="place",
    )(points)


def in_place_squares(points):
    return pl.pallas_call(
        squares_kernel,
        out_shape=(
            jax.ShapeDtypeStruct(points.shape, jnp.bfloat16),
            jax.ShapeDtypeStruct(SMALL, F32),
        ),
        in_specs=[VMEM],
        out_specs=(VMEM, VMEM),
        input_output_aliases={0: 0},
        compiler_params=PARAMS,
        cost_estimate=COST,
        name="in_place_squares",
    )(points)


def call(kernel, shapes, scratch, *args):
    return pl.pallas_call(
        kernel,
        out_shape=[jax.ShapeDtypeStruct(shape, F32) for shape in shapes],
        in_specs=[VMEM] * len(args),
        out_specs=[VMEM] * len(shapes),
        scratch_shapes=scratch,
        compiler_params=PARAMS,
        cost_estimate=COST,
        name=kernel.__name__,
    )(*args)


def products(a, b):
    return SCALE * lax.dot_general(a, b, (((1,), (1,)), ((), ())), preferred_element_type=F32)


def squares(points):
    return jnp.sum(jnp.square(points.astype(F32)), axis=1).reshape(-1, LANES)


def core_first(values):
    return values.reshape(NY, NC, -1).transpose(1, 0, 2).reshape(SMALL)


def y_first(values):
    return values.reshape(NC, NY, -1).transpose(1, 0, 2).reshape(-1)


def local(source_points, target_points, source_logmass, target_logmass):
    rows, cols = lax.axis_size("row"), lax.axis_size("col")
    masses = core_first(source_logmass * LOG2E), (target_logmass * LOG2E).reshape(SMALL)
    mine, other, target, masses = gather_points(source_points, target_points, masses)
    source_mass, target_mass = masses
    other, other_sq = place(other)
    source_sq = jnp.concatenate([squares(mine), other_sq], axis=0)
    target, other, source_sq = lax.optimization_barrier((target, other, source_sq))
    target, target_sq = in_place_squares(target)
    tiles = products(mine, target), products(other, target)
    (part,) = call(first_kernel, [(cols,) + SMALL], [WIDE], target_mass, target_sq, *tiles)
    for step in range(ITERS):
        parts = lax.all_to_all(part, "col", 0, 0)
        part, source_potential = call(
            target_kernel, [(rows,) + SMALL, SMALL], [TALL], parts, source_mass, source_sq, *tiles
        )
        parts = lax.all_to_all(part, "row", 0, 0)
        if step < ITERS - 1:
            (part,) = call(source_kernel, [(cols,) + SMALL], [WIDE], parts, target_mass, *tiles)
    (target_potential,) = call(last_kernel, [SMALL], [], parts, target_sq)
    return y_first(source_potential), target_potential.reshape(-1)


def solution(mesh):
    in_specs = (P(("row", "col"), None), P(("col", "row"), None), P("row"), P("col"))
    out_specs = (P("row"), P("col"))
    return jax.shard_map(local, mesh=mesh, in_specs=in_specs, out_specs=out_specs, check_vma=False)
```

```python
import math

import jax
import jax.numpy as jnp
from jax import lax
from jax.experimental import pallas as pl
from jax.experimental.pallas import tpu as pltpu
from jax.sharding import PartitionSpec as P

ITERS = 3
EPSILON = 0.05
LOG2E = math.log2(math.e)
SCALE = 2.0 / EPSILON * LOG2E
BACK = EPSILON / LOG2E
NX, NZ, NY, NC = 4, 8, 8, 2
N = 1024
LANES = 128
GROUPS = N // LANES
F32 = jnp.float32
SMALL = (GROUPS, LANES)


def move_col(values, place):
    pairs = []
    for y in range(NY):
        for core in range(NC):
            to_y, to_core = place(y, core)
            pairs.append((y * NC + core, to_y % NY * NC + to_core))
    return lax.ppermute(values, "col", pairs)


def move_y(values, steps):
    return move_col(values, lambda y, core: (y + steps, core))


def ring_step(ahead, back):
    return move_y(ahead, 1), move_y(back, -1)


def spread(values, count, lines):
    copies = pl.pallas_call(
        copies_kernel,
        out_shape=jax.ShapeDtypeStruct((count,) + values.shape, values.dtype),
        in_specs=[HBM],
        out_specs=HBM,
        scratch_shapes=[pltpu.SemaphoreType.DMA((count,))],
        compiler_params=PARAMS,
        cost_estimate=pl.CostEstimate(flops=0, bytes_accessed=2**22, transcendentals=0),
        name="copies",
    )(values)
    out = lax.all_to_all(copies, "row", 0, 0, axis_index_groups=lines)
    return out.reshape((-1,) + values.shape[1:])


def gather_points(source_points, target_points, masses):
    along_z = [[x * NZ + z for z in range(NZ)] for x in range(NX)]
    along_x = [[x * NZ + z for x in range(NX)] for z in range(NZ)]
    line = spread(target_points, NZ, along_z)
    before, after = ring_step(source_points, source_points)
    before, after, line, masses = lax.optimization_barrier((before, after, line, masses))
    target = spread(line, NX, along_x)
    half = source_points.shape[0] // 2
    two_before = move_y(jnp.concatenate([source_points, before], axis=0), 2)
    two_after = move_y(jnp.concatenate([source_points, after], axis=0), -2)
    far_low, far_high = move_y(after[:half], -3), move_y(before[half:], 3)
    mine = assemble([source_points, before, after, two_before, two_after, far_low, far_high])
    other = move_col(mine, lambda y, core: (y, 1 - core))
    return mine, other, target, masses


def assemble_kernel(*refs):
    pieces, (out, sems) = refs[:7], refs[7:]
    rows = pieces[0].shape[0]
    half = rows // 2
    moves = [(0, 0, 0, 0), (1, 0, -1, 0), (2, 0, 1, 0), (3, 0, -2, 0), (3, rows, -3, 0)]
    moves += [(4, 0, 2, 0), (4, rows, 3, 0), (5, 0, 4, 0), (6, 0, 4, half)]
    y = lax.axis_index("col") // NC
    made = []
    for k, (piece, first, place, offset) in enumerate(moves):
        size = min(rows, pieces[piece].shape[0])
        start = pl.multiple_of((y + place + NY) % NY * rows + offset, half)
        made.append(
            pltpu.make_async_copy(
                pieces[piece].at[pl.ds(first, size)], out.at[pl.ds(start, size)], sems.at[k]
            )
        )
        made[-1].start()
    for copy in made:
        copy.wait()


def copies_kernel(values, out, sems):
    made = [
        pltpu.make_async_copy(values, out.at[k], sems.at[k]) for k in range(out.shape[0])
    ]
    for copy in made:
        copy.start()
    for copy in made:
        copy.wait()


def place_kernel(points, out, squares, sems):
    made = []
    groups = squares.shape[0]
    for r in range(groups):
        rows = pl.ds(r * LANES, LANES)
        made.append(pltpu.make_async_copy(points.at[rows], out.at[rows], sems.at[r]))
        made[-1].start()
    sums = []
    for r in range(groups):
        made[r].wait()
        square = jnp.square(out[pl.ds(r * LANES, LANES), :].astype(F32))
        total = jnp.sum(square, axis=1, keepdims=True)
        sums.append(jnp.broadcast_to(total, (LANES, LANES)).T[0:1])
    squares[...] = jnp.concatenate(sums, axis=0)


def squares_kernel(points, same, squares):
    sums = []
    for r in range(GROUPS):
        square = jnp.square(points[pl.ds(r * LANES, LANES), :].astype(F32))
        total = jnp.sum(square, axis=1, keepdims=True)
        sums.append(jnp.broadcast_to(total, (LANES, LANES)).T[0:1])
    squares[...] = jnp.concatenate(sums, axis=0)


def columns(values, side):
    for r in range(GROUPS):
        side[pl.ds(r * LANES, LANES), :] = jnp.broadcast_to(values[r : r + 1], (LANES, LANES)).T


def by_core(values):
    swapped = jnp.concatenate([values[GROUPS // 2 :], values[: GROUPS // 2]], axis=0)
    core = lax.axis_index("col") % NC
    return jnp.where(core == 1, swapped, values)


def merge_all(parts):
    top = jnp.max(parts, axis=0)
    return top + jnp.log2(jnp.sum(jnp.exp2(parts - top[None]), axis=0))


def over_targets(values, mine, other, part, flat):
    for r in range(GROUPS):
        flat[:, pl.ds(r * LANES, LANES)] = jnp.broadcast_to(values[r : r + 1], SMALL)
    rows = []
    for scaled in (mine, other):
        for r in range(GROUPS // NC):
            tile = scaled[pl.ds(r * LANES, LANES), :] + flat[0:1, :]
            top = jnp.max(tile, axis=1, keepdims=True)
            log = top + jnp.log2(jnp.sum(jnp.exp2(tile - top), axis=1, keepdims=True))
            rows.append(jnp.broadcast_to(log, (LANES, LANES)).T[0:1])
    part[...] = jnp.broadcast_to(by_core(jnp.concatenate(rows, axis=0))[None], part.shape)


def first_kernel(mass, squares, mine, other, part, flat):
    over_targets(mass[...] - squares[...] * (1.0 / BACK), mine, other, part, flat)


def source_kernel(parts, mass, mine, other, part, flat):
    over_targets(mass[...] - merge_all(parts[...]), mine, other, part, flat)


def target_kernel(parts, mass, squares, mine, other, part, potential, side):
    log = merge_all(parts[...])
    potential[...] = by_core(squares[...]) - BACK * log
    columns(by_core(mass[...] - log), side)
    rows = []
    for r in range(GROUPS):
        at = pl.ds(r * LANES, LANES)
        tile = jnp.concatenate([mine[:, at], other[:, at]], axis=0) + side[...]
        top = jnp.max(tile, axis=0, keepdims=True)
        rows.append(top + jnp.log2(jnp.sum(jnp.exp2(tile - top), axis=0, keepdims=True)))
    part[...] = jnp.broadcast_to(jnp.concatenate(rows, axis=0)[None], part.shape)


def last_kernel(parts, squares, potential):
    potential[...] = squares[...] - BACK * merge_all(parts[...])


VMEM = pl.BlockSpec(memory_space=pltpu.VMEM)
HBM = pl.BlockSpec(memory_space=pltpu.HBM)
PARAMS = pltpu.CompilerParams(vmem_limit_bytes=16 * 2**20)
COST = pl.CostEstimate(flops=6 * N * N, bytes_accessed=4 * N * N, transcendentals=N * N)


def assemble(pieces):
    rows, depth = pieces[0].shape
    return pl.pallas_call(
        assemble_kernel,
        out_shape=jax.ShapeDtypeStruct((NY * rows, depth), jnp.bfloat16),
        in_specs=[HBM] * len(pieces),
        out_specs=VMEM,
        scratch_shapes=[pltpu.SemaphoreType.DMA((9,))],
        compiler_params=PARAMS,
        cost_estimate=pl.CostEstimate(flops=0, bytes_accessed=2**22, transcendentals=0),
        name="assemble",
    )(*pieces)


WIDE = pltpu.VMEM((GROUPS, N), F32)
TALL = pltpu.VMEM((N, LANES), F32)


def place(points):
    groups = points.shape[0] // LANES
    return pl.pallas_call(
        place_kernel,
        out_shape=(
            jax.ShapeDtypeStruct(points.shape, jnp.bfloat16),
            jax.ShapeDtypeStruct((groups, LANES), F32),
        ),
        in_specs=[HBM],
        out_specs=(VMEM, VMEM),
        scratch_shapes=[pltpu.SemaphoreType.DMA((groups,))],
        compiler_params=PARAMS,
        cost_estimate=pl.CostEstimate(
            flops=2 * points.size, bytes_accessed=2 * points.size, transcendentals=0
        ),
        name="place",
    )(points)


def in_place_squares(points):
    return pl.pallas_call(
        squares_kernel,
        out_shape=(
            jax.ShapeDtypeStruct(points.shape, jnp.bfloat16),
            jax.ShapeDtypeStruct(SMALL, F32),
        ),
        in_specs=[VMEM],
        out_specs=(VMEM, VMEM),
        input_output_aliases={0: 0},
        compiler_params=PARAMS,
        cost_estimate=COST,
        name="in_place_squares",
    )(points)


def call(kernel, shapes, scratch, *args):
    return pl.pallas_call(
        kernel,
        out_shape=[jax.ShapeDtypeStruct(shape, F32) for shape in shapes],
        in_specs=[VMEM] * len(args),
        out_specs=[VMEM] * len(shapes),
        scratch_shapes=scratch,
        compiler_params=PARAMS,
        cost_estimate=COST,
        name=kernel.__name__,
    )(*args)


def products(a, b):
    return SCALE * lax.dot_general(a, b, (((1,), (1,)), ((), ())), preferred_element_type=F32)


def squares(points):
    return jnp.sum(jnp.square(points.astype(F32)), axis=1).reshape(-1, LANES)


def core_first(values):
    return values.reshape(NY, NC, -1).transpose(1, 0, 2).reshape(SMALL)


def y_first(values):
    return values.reshape(NC, NY, -1).transpose(1, 0, 2).reshape(-1)


def local(source_points, target_points, source_logmass, target_logmass):
    rows, cols = lax.axis_size("row"), lax.axis_size("col")
    masses = core_first(source_logmass * LOG2E), (target_logmass * LOG2E).reshape(SMALL)
    mine, other, target, masses = gather_points(source_points, target_points, masses)
    source_mass, target_mass = masses
    target, other, mine_sq = lax.optimization_barrier((target, other, squares(mine)))
    other, other_sq = place(other)
    target, target_sq = in_place_squares(target)
    source_sq = jnp.concatenate([mine_sq, other_sq], axis=0)
    target, other, source_sq = lax.optimization_barrier((target, other, source_sq))
    tiles = products(mine, target), products(other, target)
    (part,) = call(first_kernel, [(cols,) + SMALL], [WIDE], target_mass, target_sq, *tiles)
    for step in range(ITERS):
        parts = lax.all_to_all(part, "col", 0, 0)
        part, source_potential = call(
            target_kernel, [(rows,) + SMALL, SMALL], [TALL], parts, source_mass, source_sq, *tiles
        )
        parts = lax.all_to_all(part, "row", 0, 0)
        if step < ITERS - 1:
            (part,) = call(source_kernel, [(cols,) + SMALL], [WIDE], parts, target_mass, *tiles)
    (target_potential,) = call(last_kernel, [SMALL], [], parts, target_sq)
    return y_first(source_potential), target_potential.reshape(-1)


def solution(mesh):
    in_specs = (P(("row", "col"), None), P(("col", "row"), None), P("row"), P("col"))
    out_specs = (P("row"), P("col"))
    return jax.shard_map(local, mesh=mesh, in_specs=in_specs, out_specs=out_specs, check_vma=False)
```
